32 devices in a mesh: tiles: 8 (over z, y), nests: 4 (over x, core).
Axes of the slice: x: 2, y: 2, z: 4, core: 2. Of those that a mesh axis runs over, the one named last changes fastest.
Arguments:
- parent: float32 [512, 1024, 128], P('tiles', 'nests'), may hold values from -6 to 6
- nest_state: float32 [4, 32, 128, 128], P('nests', 'tiles'), may hold values from -6 to 6
- parent_mix: float32 [128, 128], replicated, may hold values from -0.24 to 0.24
- nest_mix: float32 [128, 128], replicated, may hold values from -0.24 to 0.24
- courant: float32 [2, 128], replicated, may hold values from 0.05 to 0.45
- nest_pos: int32 [4, 2], P('nests'), may hold values from 0 to 2882, as said below
Outputs:
- parent_out: float32 [512, 1024, 128], P('tiles', 'nests')
- nest_out: float32 [4, 32, 128, 128], P('nests', 'tiles')
The draws below stay inside these ranges and needn't reach their ends.
Inputs may be any that keep to these rules, and one draw needn't show every extreme that they name: nest_pos[n] = (3 i + a, 3 q + c) with a, c in 0..2, i <= 499, and n * 256 <= q <= (n + 1) * 256 - 64: nest n reads and feeds only parent columns of the n-th group of 256 columns.
All inputs are finite; a program needn't handle non-finite values.
Results may differ from the reference program's by a relative error of at most 0.0003.
Values sent between devices are 32-bit elements; how exact they have to be, the bound alone decides.
A program may use at most 128 MiB of HBM per device.

```python
import jax
import jax.numpy as jnp
from jax import lax

COL = 128
TY = 256
BLK = 64
NY = 128
STEPS = 3
PX = 512
PY = 1024
NX = 32
WIN = 13
NESTS = 4


def draw_nest_pos(key, part):
    need = (NX + 1) // 3 + 2
    start_rows = jax.random.randint(jax.random.fold_in(key, 101), (NESTS,), 0, PX - need + 1).astype(jnp.int32)
    phase_x = jax.random.randint(jax.random.fold_in(key, 102), (NESTS,), 0, 3).astype(jnp.int32)
    within = jax.random.randint(jax.random.fold_in(key, 103), (NESTS,), 0, TY - BLK + 1).astype(jnp.int32)
    phase_y = jax.random.randint(jax.random.fold_in(key, 104), (NESTS,), 0, 3).astype(jnp.int32)
    start_rows = start_rows.at[0].set(PX - need).at[1].set(0)
    phase_x = phase_x.at[0].set(2).at[1].set(0)
    within = within.at[NESTS - 1].set(TY - BLK)
    phase_y = phase_y.at[NESTS - 1].set(2)
    corner = jnp.arange(NESTS, dtype=jnp.int32) * TY + within
    return jnp.stack([3 * start_rows + phase_x, 3 * corner + phase_y], axis=1).astype(jnp.int32)


def block_levels(own_key, shape, cuts, low, top_value):
    def one(dim, parts):
        steps = jax.random.uniform(jax.random.fold_in(jax.random.fold_in(own_key, 6), dim), (parts,), jnp.float32, low / len(cuts), top_value / len(cuts))
        return jnp.repeat(jnp.exp(steps), shape[dim] // parts).reshape((-1,) + (1,) * (len(shape) - dim - 1))

    gain = one(*cuts[0])
    for cut in cuts[1:]:
        gain = gain * one(*cut)
    return gain


def centred(rng, extent, width, limit, cuts=(), kind=jnp.bfloat16):
    entries = width * jax.random.normal(rng, extent, jnp.float32)
    if cuts:
        entries = entries * block_levels(rng, extent, cuts, -0.22, 0.18)
    return jnp.clip(entries, -limit, limit).astype(kind)


def setup_inputs(seed: int = 0) -> dict:
    keys = jax.random.split(jax.random.key(seed), 7)
    return {
        "parent": centred(keys[0], (PX, PY, COL), 1.0, 6.0, ((0, 8), (1, 4)), jnp.float32),
        "nest_state": centred(keys[1], (NESTS, NX, NY, COL), 1.0, 6.0, ((0, 4), (1, 8)), jnp.float32),
        "parent_mix": centred(keys[2], (COL, COL), 0.04, 0.24, (), jnp.float32),
        "nest_mix": centred(keys[3], (COL, COL), 0.04, 0.24, (), jnp.float32),
        "courant": jnp.clip(jax.random.uniform(keys[4], (2, COL), jnp.float32, 0.05, 0.45), 0.05, 0.45),
        "nest_pos": draw_nest_pos(jax.random.fold_in(keys[6], 71), 0),
    }


KAPPA = 0.125
HIGH = lax.Precision.HIGHEST


def parent_advance(parent, parent_mix):
    padded = jnp.pad(parent, ((1, 1), (1, 1), (0, 0)))
    beside_all = padded[2:, 1:-1] + padded[:-2, 1:-1] + padded[1:-1, 2:] + padded[1:-1, :-2]
    mixed = jnp.einsum('xyc,cd->xyd', parent, parent_mix, precision=HIGH)
    return parent + KAPPA * (beside_all - 4.0 * parent) + mixed


def nest_advance(current, upper, edge, courant, nest_mix):
    left = jnp.concatenate([edge, current[:, :-1]], axis=1)
    mixed = jnp.einsum('xyc,cd->xyd', current, nest_mix, precision=HIGH)
    return current + courant[0] * (upper - current) + courant[1] * (left - current) + mixed


def bilinear(data, anchor, rows, columns_count, block_len):
    cols = jnp.arange(columns_count, dtype=jnp.int32)
    spot = anchor[1] + cols
    near = spot // 3 - anchor[1] // 3
    frac_y = (spot % 3).astype(jnp.float32) / 3.0
    places = jnp.arange(block_len, dtype=jnp.int32)[None, :]
    zero = jnp.zeros((columns_count, block_len), jnp.float32)
    table = jnp.where(places == near[:, None], (1.0 - frac_y)[:, None] + zero, zero)
    table = table + jnp.where(places == near[:, None] + 1, frac_y[:, None] + zero, zero)
    frac_x = ((anchor[0] + rows) % 3).astype(jnp.float32) / 3.0
    upper_part = jnp.einsum('nb,xbc->xnc', table, data[:, 0], precision=HIGH)
    lower_part = jnp.einsum('nb,xbc->xnc', table, data[:, 1], precision=HIGH)
    return (1.0 - frac_x)[:, None, None] * upper_part + frac_x[:, None, None] * lower_part


def reference(parent, nest_state, parent_mix, nest_mix, courant, nest_pos):
    padded_rows = jnp.concatenate([parent, jnp.zeros((WIN, PY, COL), parent.dtype)], axis=0)
    naught = jnp.zeros((), jnp.int32)

    def one_nest(packed):
        anchor, state = packed
        top = (anchor[0] // 3).astype(jnp.int32)
        corner = (anchor[1] // 3).astype(jnp.int32)
        band = lax.dynamic_slice(padded_rows, (top, corner, naught), (WIN, BLK, COL))
        rows = jnp.arange(NX, dtype=jnp.int32)
        near_row = (anchor[0] + rows) // 3 - top
        data = jnp.stack([band[near_row], band[near_row + 1]], axis=1)
        interp = bilinear(data, anchor, rows, NY, BLK)
        start = 0.5 * (state + interp)
        edge = start[:, :1]
        current = start
        for step in range(STEPS):
            upper = jnp.concatenate([start[:1], current[:-1]], axis=0)
            current = nest_advance(current, upper, edge, courant, nest_mix)
        return current

    nest_out = lax.map(one_nest, (nest_pos, nest_state))
    parent_new = parent_advance(parent, parent_mix)

    fb_rows = (NX + 2) // 3
    fb_cols = (NY + 2) // 3
    parent_out = parent_new
    for nest_index in range(NESTS):
        anchor_x = nest_pos[nest_index, 0]
        anchor_y = nest_pos[nest_index, 1]
        xs = (-anchor_x) % 3 + 3 * jnp.arange(fb_rows, dtype=jnp.int32)
        ys = (-anchor_y) % 3 + 3 * jnp.arange(fb_cols, dtype=jnp.int32)
        valid = (xs < NX)[:, None] & (ys < NY)[None, :]
        values = nest_out[nest_index][jnp.clip(xs, 0, NX - 1)][:, jnp.clip(ys, 0, NY - 1)]
        prow = (anchor_x + xs) // 3
        pcol = (anchor_y + ys) // 3
        old = parent_new[jnp.clip(prow, 0, PX - 1)[:, None], jnp.clip(pcol, 0, PY - 1)[None, :]]
        diff = jnp.where(valid[..., None], 0.5 * (values - old), 0.0)
        row_index = jnp.where(valid, prow[:, None], PX)
        col_index = jnp.broadcast_to(pcol[None, :], valid.shape)
        parent_out = parent_out.at[row_index, col_index].add(diff, mode="drop")
    return parent_out, nest_out
```

```python
import functools

import jax
import jax.numpy as jnp
from jax import lax
from jax.experimental import pallas as pl
from jax.experimental.pallas import tpu as pltpu
from jax.sharding import PartitionSpec as P

STEPS = 3
KAPPA = 0.125
HIGH = lax.Precision.HIGHEST
MESH = pl.DeviceIdType.MESH
LANES = 8
ROWS = 8
VMEM_LIMIT = 48 * 1024 * 1024


def split_operator(mix):
    high = mix.astype(jnp.bfloat16)
    low = (mix - high.astype(jnp.float32)).astype(jnp.bfloat16)
    upper = jnp.concatenate([high, low], axis=1)
    lower = jnp.concatenate([high, jnp.zeros_like(low)], axis=1)
    return jnp.concatenate([upper, lower], axis=0)


def apply_operator(values, operator):
    width = values.shape[-1]
    high = values.astype(jnp.bfloat16)
    low = (values - high.astype(jnp.float32)).astype(jnp.bfloat16)
    both = jnp.dot(
        jnp.concatenate([high, low], axis=1), operator, preferred_element_type=jnp.float32
    )
    return both[:, :width] + both[:, width:]


def hat(distance):
    return jnp.maximum(3 - jnp.abs(distance), 0).astype(jnp.float32) * (1.0 / 3.0)


def exchange_kernel(
    nt, nn, lo_count, pos, band, state, edges, mix, courant, parent,
    nest_out, feed, above, below, beside,
    arrived, reduced, rows, halo, start, current,
    send1, recv1, send2, recv2, send3, recv3, send4, recv4,
):
    t = lax.axis_index("tiles")
    n = lax.axis_index("nests")
    nest_rows, nest_cols, width = state.shape
    win = band.shape[0]
    groups = band.shape[1] // LANES
    count = rows.shape[1]
    relay0 = (nt - groups) // 2
    tile_rows = parent.shape[0]

    def low_row(tile):
        return jnp.clip((tile * nest_rows - STEPS + 3) // 3 - 1, 0, win - count)

    def remote(src, dst, send, recv, tile, nest):
        return pltpu.make_async_remote_copy(
            src_ref=src, dst_ref=dst, send_sem=send, recv_sem=recv,
            device_id=(tile, nest), device_id_type=MESH,
        )

    barrier = pltpu.get_barrier_semaphore()
    for step in range(1, nt):
        pl.semaphore_signal(
            barrier, inc=1, device_id=(lax.rem(t + step, nt), n), device_id_type=MESH
        )

    @pl.when(n > 0)
    def _():
        pl.semaphore_signal(barrier, inc=1, device_id=(t, n - 1), device_id_type=MESH)

    @pl.when(n < nn - 1)
    def _():
        pl.semaphore_signal(barrier, inc=1, device_id=(t, n + 1), device_id_type=MESH)

    peers = nt - 1 + (n > 0).astype(jnp.int32) + (n < nn - 1).astype(jnp.int32)
    pl.semaphore_wait(barrier, peers)

    def gather_copy(g):
        return remote(
            band.at[:, pl.ds(g * LANES, LANES)], arrived.at[t], send1.at[g], recv1.at[t],
            relay0 + g, n,
        )

    for g in range(groups):
        @pl.when(t != relay0 + g)
        def _():
            gather_copy(g).start()

    def halo_copy():
        return remote(
            state.at[pl.ds(nest_rows - STEPS, STEPS)], halo, send3.at[0], recv3.at[0], t + 1, n
        )

    def down_copy():
        return remote(parent.at[tile_rows - 1], above, send3.at[1], recv3.at[1], t + 1, n)

    def up_copy():
        return remote(parent.at[0], below, send3.at[2], recv3.at[2], t - 1, n)

    def right_copy():
        return remote(edges.at[1], beside.at[0], send3.at[3], recv3.at[3], t, n + 1)

    def left_copy():
        return remote(edges.at[0], beside.at[1], send3.at[4], recv3.at[4], t, n - 1)

    @pl.when(t < nt - 1)
    def _():
        halo_copy().start()
        down_copy().start()

    @pl.when(t > 0)
    def _():
        up_copy().start()

    @pl.when(n < nn - 1)
    def _():
        right_copy().start()

    @pl.when(n > 0)
    def _():
        left_copy().start()

    @pl.when(t == 0)
    def _():
        halo[...] = jnp.zeros_like(halo)
        above[...] = jnp.zeros_like(above)

    @pl.when(t == nt - 1)
    def _():
        below[...] = jnp.zeros_like(below)

    @pl.when(n == 0)
    def _():
        beside[0] = jnp.zeros(beside.shape[1:], jnp.float32)

    @pl.when(n == nn - 1)
    def _():
        beside[1] = jnp.zeros(beside.shape[1:], jnp.float32)

    is_relay = (t >= relay0) & (t < relay0 + groups)

    def spread_copy(r):
        return remote(
            reduced.at[pl.ds(low_row(r), count)], rows.at[t - relay0], send2.at[r],
            recv2.at[t - relay0], r, n,
        )

    def arrive_copy(s):
        return remote(
            band.at[:, pl.ds(0, LANES)], arrived.at[s], send1.at[0], recv1.at[s], s, n
        )

    for g in range(groups):
        @pl.when(t == relay0 + g)
        def _():
            reduced[...] = band[:, g * LANES:(g + 1) * LANES]

    for s in range(nt):
        @pl.when(is_relay & (t != s))
        def _():
            arrive_copy(s).wait_recv()
            reduced[...] += arrived[s]

    for r in range(nt):
        @pl.when(is_relay & (t != r))
        def _():
            spread_copy(r).start()

    for g in range(groups):
        @pl.when(t == relay0 + g)
        def _():
            rows[g] = reduced[pl.ds(low_row(t), count)]

    operator = split_operator(mix[...])
    shift_x = lax.rem(pos[0, 0], 3)
    shift_y = lax.rem(pos[0, 1], 3)
    span = (nest_cols, groups * LANES)
    table = hat(
        shift_y + lax.broadcasted_iota(jnp.int32, span, 0)
        - 3 * lax.broadcasted_iota(jnp.int32, span, 1)
    )
    first = t == 0

    @pl.when(t > 0)
    def _():
        halo_copy().wait_recv()

    for g in range(groups):
        @pl.when(t != relay0 + g)
        def _():
            remote(
                reduced.at[pl.ds(0, count)], rows.at[g], send2.at[0], recv2.at[g], t, n
            ).wait_recv()

    lines = [
        jnp.dot(
            table, rows[:, i].reshape(groups * LANES, width),
            precision=HIGH, preferred_element_type=jnp.float32,
        )
        for i in range(count)
    ]
    base = t * nest_rows
    lowest = low_row(t)
    total = nest_rows + STEPS
    for k in range(total):
        interp = None
        for i in range(count):
            weight = hat(shift_x + base - STEPS + k - 3 * (lowest + i))
            term = weight * lines[i]
            interp = term if interp is None else interp + term
        own = halo[k] if k < STEPS else state[k - STEPS]
        value = 0.5 * (own + interp)
        start[k] = value
        current[k] = value

    along_x = courant[0:1]
    along_y = courant[1:2]
    at_edge = lax.broadcasted_iota(jnp.int32, (nest_cols, width), 0) == 0
    for step in range(STEPS):
        for k in range(total - 1, step, -1):
            value = current[k]
            upper = current[k - 1]
            if k == STEPS:
                upper = jnp.where(first, start[k], upper)
            left = jnp.where(at_edge, start[k, 0:1], pltpu.roll(value, 1, 0))
            current[k] = (
                value + along_x * (upper - value) + along_y * (left - value)
                + apply_operator(value, operator)
            )

    lead_x = lax.rem(3 - lax.rem(shift_x + base, 3), 3)
    lead_y = lax.rem(3 - shift_y, 3)
    cells = feed.shape[2]
    pick = (
        lax.broadcasted_iota(jnp.int32, (cells, nest_cols), 1)
        == lead_y + 3 * lax.broadcasted_iota(jnp.int32, (cells, nest_cols), 0)
    ).astype(jnp.float32)
    r0, r1, r2, r3 = (current[STEPS + i] for i in range(nest_rows))
    chosen = jnp.where(lead_x == 0, r0, jnp.where(lead_x == 1, r1, r2))
    feed[t, 0] = jnp.dot(pick, chosen, precision=HIGH, preferred_element_type=jnp.float32)
    feed[t, 1] = jnp.dot(pick, r3, precision=HIGH, preferred_element_type=jnp.float32)

    hi_count = nt // lo_count
    hi, lo = t // lo_count, lax.rem(t, lo_count)

    def feed_copy(source, target, slot):
        return remote(feed.at[source], feed.at[source], send4.at[slot], recv4.at[source], target, n)

    sends = []
    for step in range(1, hi_count):
        sends.append(feed_copy(t, lax.rem(hi + step, hi_count) * lo_count + lo, len(sends)))
        sends[-1].start()
    for step in range(1, lo_count):
        sends.append(feed_copy(t, hi * lo_count + lax.rem(lo + step, lo_count), len(sends)))
        sends[-1].start()

    nest_out[...] = current[STEPS:]

    for step in range(1, hi_count):
        source = lax.rem(hi + step, hi_count) * lo_count + lo
        feed_copy(source, t, 0).wait_recv()
        for across in range(1, lo_count):
            target = hi * lo_count + lax.rem(lo + across, lo_count)
            sends.append(feed_copy(source, target, len(sends)))
            sends[-1].start()
    for across in range(1, lo_count):
        for step in range(hi_count):
            source = lax.rem(hi + step, hi_count) * lo_count + lax.rem(lo + across, lo_count)
            feed_copy(source, t, 0).wait_recv()

    @pl.when(t > 0)
    def _():
        down_copy().wait_recv()

    @pl.when(t < nt - 1)
    def _():
        up_copy().wait_recv()

    @pl.when(n > 0)
    def _():
        right_copy().wait_recv()

    @pl.when(n < nn - 1)
    def _():
        left_copy().wait_recv()

    for copy in sends:
        copy.wait_send()
    for g in range(groups):
        @pl.when(t != relay0 + g)
        def _():
            gather_copy(g).wait_send()
    for r in range(nt):
        @pl.when(is_relay & (t != r))
        def _():
            spread_copy(r).wait_send()

    @pl.when(t < nt - 1)
    def _():
        halo_copy().wait_send()
        down_copy().wait_send()

    @pl.when(t > 0)
    def _():
        up_copy().wait_send()

    @pl.when(n < nn - 1)
    def _():
        right_copy().wait_send()

    @pl.when(n > 0)
    def _():
        left_copy().wait_send()


def parent_kernel(nest_rows, nest_total, nest_cols, place, block, over, under, above, below,
                  beside, mix, feed, out, operator):
    step = pl.program_id(0)
    last = pl.num_programs(0) - 1
    lines, cols, width = block.shape

    @pl.when(step == 0)
    def _():
        operator[...] = split_operator(mix[...])

    column = lax.broadcasted_iota(jnp.int32, (cols, width), 0)
    weights = operator[...]
    for i in range(lines):
        value = block[i]
        if i == 0:
            up = jnp.where(step == 0, above[...], over[0])
        else:
            up = block[i - 1]
        if i == lines - 1:
            down = jnp.where(step == last, below[...], under[0])
        else:
            down = block[i + 1]
        row = step * lines + i
        left = jnp.where(column == 0, beside[0, pl.ds(row, 1)], pltpu.roll(value, 1, 0))
        right = jnp.where(
            column == cols - 1, beside[1, pl.ds(row, 1)], pltpu.roll(value, cols - 1, 0)
        )
        out[i] = (
            value + KAPPA * ((up + down + right + left) - 4.0 * value)
            + apply_operator(value, weights)
        )

    top, lead_x, first_col, lead_y = place[0], place[1], place[2], place[3]
    slots = feed.shape[1]
    cells = feed.shape[2]
    window = cells + 8
    base_col = pl.multiple_of(first_col // 8 * 8, 8)
    offset = first_col - base_col
    limit = (nest_cols - lead_y + 2) // 3
    for i in range(lines):
        x = lead_x + 3 * (step * lines + i - top)

        @pl.when((x >= 0) & (x < nest_total))
        def _():
            sender = x // nest_rows
            slot = (x - sender * nest_rows) // 3
            cell = lax.broadcasted_iota(jnp.int32, (window, width), 0) - offset
            fed = jnp.concatenate([feed[sender, slot], jnp.zeros((8, width), jnp.float32)], axis=0)
            fed = pltpu.roll(fed, offset, 0)
            old = out[i, pl.ds(base_col, window)]
            new = jnp.where((cell >= 0) & (cell < limit), old + 0.5 * (fed - old), old)
            out[i, pl.ds(base_col, window)] = new


def shards(nt, nn, parent, nest_state, parent_mix, nest_mix, courant, nest_pos):
    tile_rows, tile_cols, width = parent.shape
    _, nest_rows, nest_cols, _ = nest_state.shape
    nest_total = nest_rows * nt
    win = (nest_total + 1) // 3 + 2
    need = (nest_cols + 1) // 3 + 2
    span = -(-need // LANES) * LANES
    groups = span // LANES
    count = -(-(nest_rows + STEPS + 1) // 3) + 2
    fb_cols = -(-((nest_cols + 2) // 3) // LANES) * LANES
    lo_count = nt // 4
    slots = (nest_rows + 2) // 3
    t = lax.axis_index("tiles")
    n = lax.axis_index("nests")
    anchor = nest_pos[0]
    local = anchor[0] // 3 - t * tile_rows
    corner = anchor[1] // 3 - n * tile_cols
    begin = jnp.clip(local, 0, tile_rows - win)
    strip = lax.dynamic_slice(parent, (begin, corner, 0), (win, span, width))
    strip = jnp.pad(strip, ((win, win), (0, 0), (0, 0)))
    move = jnp.clip(local - begin, -win, win) + win
    band = lax.dynamic_slice(strip, (move, 0, 0), (win, span, width))
    edges = jnp.stack([parent[:, 0], parent[:, -1]])
    vmem = pl.BlockSpec(memory_space=pltpu.VMEM)
    f32 = jnp.float32
    dma = pltpu.SemaphoreType.DMA
    nest_out, feed, above, below, beside = pl.pallas_call(
        functools.partial(exchange_kernel, nt, nn, lo_count),
        out_shape=(
            jax.ShapeDtypeStruct((nest_rows, nest_cols, width), f32),
            jax.ShapeDtypeStruct((nt, slots, fb_cols, width), f32),
            jax.ShapeDtypeStruct((tile_cols, width), f32),
            jax.ShapeDtypeStruct((tile_cols, width), f32),
            jax.ShapeDtypeStruct((2, tile_rows, width), f32),
        ),
        in_specs=[
            pl.BlockSpec(memory_space=pltpu.SMEM), vmem, vmem, vmem, vmem, vmem,
            pl.BlockSpec(memory_space=pl.ANY),
        ],
        out_specs=(vmem,) * 5,
        scratch_shapes=[
            pltpu.VMEM((nt, win, LANES, width), f32),
            pltpu.VMEM((win, LANES, width), f32),
            pltpu.VMEM((groups, count, LANES, width), f32),
            pltpu.VMEM((STEPS, nest_cols, width), f32),
            pltpu.VMEM((nest_rows + STEPS, nest_cols, width), f32),
            pltpu.VMEM((nest_rows + STEPS, nest_cols, width), f32),
            dma((groups,)), dma((nt,)), dma((nt,)), dma((groups,)),
            dma((5,)), dma((5,)), dma((nt - 1,)), dma((nt,)),
        ],
        compiler_params=pltpu.CompilerParams(
            collective_id=0, has_side_effects=True, vmem_limit_bytes=VMEM_LIMIT
        ),
        name="nest_exchange",
    )(nest_pos, band, nest_state[0], edges, nest_mix, courant, parent)

    lead_x = -anchor[0] % 3
    lead_y = -anchor[1] % 3
    place = jnp.stack([
        (anchor[0] + lead_x) // 3 - t * tile_rows,
        lead_x,
        (anchor[1] + lead_y) // 3 - n * tile_cols,
        lead_y,
    ]).astype(jnp.int32)
    steps = tile_rows // ROWS
    whole = lambda *shape: pl.BlockSpec(shape, lambda i, place: (0,) * len(shape))
    line = (1, tile_cols, width)
    parent_out = pl.pallas_call(
        functools.partial(parent_kernel, nest_rows, nest_total, nest_cols),
        out_shape=jax.ShapeDtypeStruct(parent.shape, f32),
        grid_spec=pltpu.PrefetchScalarGridSpec(
            num_scalar_prefetch=1,
            grid=(steps,),
            in_specs=[
                pl.BlockSpec((ROWS, tile_cols, width), lambda i, place: (i, 0, 0)),
                pl.BlockSpec(line, lambda i, place: (jnp.maximum(i * ROWS - 1, 0), 0, 0)),
                pl.BlockSpec(
                    line, lambda i, place: (jnp.minimum(i * ROWS + ROWS, tile_rows - 1), 0, 0)
                ),
                whole(tile_cols, width),
                whole(tile_cols, width),
                whole(2, tile_rows, width),
                whole(width, width),
                whole(nt, slots, fb_cols, width),
            ],
            out_specs=pl.BlockSpec((ROWS, tile_cols, width), lambda i, place: (i, 0, 0)),
            scratch_shapes=[pltpu.VMEM((2 * width, 2 * width), jnp.bfloat16)],
        ),
        compiler_params=pltpu.CompilerParams(vmem_limit_bytes=VMEM_LIMIT),
        name="parent_step",
    )(place, parent, parent, parent, above, below, beside, parent_mix, feed)
    return parent_out, nest_out[None]


def solution(mesh):
    placed = (
        P("tiles", "nests", None),
        P("nests", "tiles", None, None),
        P(),
        P(),
        P(),
        P("nests", None),
    )
    return jax.shard_map(
        functools.partial(shards, mesh.shape["tiles"], mesh.shape["nests"]),
        mesh=mesh,
        in_specs=placed,
        out_specs=(P("tiles", "nests", None), P("nests", "tiles", None, None)),
        check_vma=False,
    )
```

```python
import functools

import jax
import jax.numpy as jnp
from jax import lax
from jax.experimental import pallas as pl
from jax.experimental.pallas import tpu as pltpu
from jax.sharding import PartitionSpec as P

STEPS = 3
KAPPA = 0.125
HIGH = lax.Precision.HIGHEST
MESH = pl.DeviceIdType.MESH
LANES = 8
ROWS = 8
CHUNK = 4
PAD = 8
VMEM_LIMIT = 56 * 1024 * 1024


def split_operator(mix):
    high = mix.astype(jnp.bfloat16)
    low = (mix - high.astype(jnp.float32)).astype(jnp.bfloat16)
    upper = jnp.concatenate([high, low], axis=1)
    lower = jnp.concatenate([high, jnp.zeros_like(low)], axis=1)
    return jnp.concatenate([upper, lower], axis=0)


def apply_operator(values, operator):
    width = values.shape[-1]
    high = values.astype(jnp.bfloat16)
    low = (values - high.astype(jnp.float32)).astype(jnp.bfloat16)
    both = jnp.dot(
        jnp.concatenate([high, low], axis=1), operator, preferred_element_type=jnp.float32
    )
    return both[:, :width] + both[:, width:]


def hat(distance):
    return jnp.maximum(3 - jnp.abs(distance), 0).astype(jnp.float32) * (1.0 / 3.0)


def exchange_kernel(
    nt, nn, lo_count, pos, parent_hbm, state_hbm, pmix_hbm, nmix_hbm, courant_hbm,
    nest_out, feed, parent_new,
    held, fresh, band, edges, above, below, beside, state, pmix, nmix, courant,
    arrived, reduced, rows, halo, start, current,
    load, store, send1, recv1, send2, recv2, send3, recv3, send4, recv4,
):
    t = lax.axis_index("tiles")
    n = lax.axis_index("nests")
    nest_rows, nest_cols, width = state.shape
    tile_rows, tile_cols, _ = fresh.shape
    win, span, _ = band.shape
    groups = span // LANES
    count = rows.shape[1]
    relay0 = (nt - groups) // 2

    def low_row(tile):
        return jnp.clip((tile * nest_rows - STEPS + 3) // 3 - 1, 0, win - count)

    def remote(src, dst, send, recv, tile, nest):
        return pltpu.make_async_remote_copy(
            src_ref=src, dst_ref=dst, send_sem=send, recv_sem=recv,
            device_id=(tile, nest), device_id_type=MESH,
        )

    loads = [
        pltpu.make_async_copy(
            parent_hbm, held.at[pl.ds(1, tile_rows), pl.ds(PAD, tile_cols)], load.at[0]
        ),
        pltpu.make_async_copy(pmix_hbm, pmix, load.at[1]),
        pltpu.make_async_copy(state_hbm.at[0], state, load.at[2]),
        pltpu.make_async_copy(nmix_hbm, nmix, load.at[3]),
        pltpu.make_async_copy(courant_hbm, courant, load.at[4]),
    ]
    for copy in loads:
        copy.start()

    barrier = pltpu.get_barrier_semaphore()
    for step in range(1, nt):
        pl.semaphore_signal(
            barrier, inc=1, device_id=(lax.rem(t + step, nt), n), device_id_type=MESH
        )

    @pl.when(n > 0)
    def _():
        pl.semaphore_signal(barrier, inc=1, device_id=(t, n - 1), device_id_type=MESH)

    @pl.when(n < nn - 1)
    def _():
        pl.semaphore_signal(barrier, inc=1, device_id=(t, n + 1), device_id_type=MESH)

    held[0] = jnp.zeros(held.shape[1:], jnp.float32)
    held[tile_rows + 1] = jnp.zeros(held.shape[1:], jnp.float32)
    strip = jnp.zeros((tile_rows, PAD, width), jnp.float32)
    held[1:tile_rows + 1, :PAD] = strip
    held[1:tile_rows + 1, PAD + tile_cols:] = strip

    @pl.when(t == 0)
    def _():
        halo[...] = jnp.zeros_like(halo)
        above[...] = jnp.zeros_like(above)

    @pl.when(t == nt - 1)
    def _():
        below[...] = jnp.zeros_like(below)

    @pl.when(n == 0)
    def _():
        beside[0] = jnp.zeros(beside.shape[1:], jnp.float32)

    @pl.when(n == nn - 1)
    def _():
        beside[1] = jnp.zeros(beside.shape[1:], jnp.float32)

    peers = nt - 1 + (n > 0).astype(jnp.int32) + (n < nn - 1).astype(jnp.int32)
    pl.semaphore_wait(barrier, peers)

    def halo_copy():
        return remote(
            state_hbm.at[0, pl.ds(nest_rows - STEPS, STEPS)], halo, send3.at[0], recv3.at[0],
            t + 1, n,
        )

    def down_copy():
        return remote(
            parent_hbm.at[tile_rows - 1], above, send3.at[1], recv3.at[1], t + 1, n
        )

    def up_copy():
        return remote(parent_hbm.at[0], below, send3.at[2], recv3.at[2], t - 1, n)

    def right_copy():
        return remote(edges.at[1], beside.at[0], send3.at[3], recv3.at[3], t, n + 1)

    def left_copy():
        return remote(edges.at[0], beside.at[1], send3.at[4], recv3.at[4], t, n - 1)

    @pl.when(t < nt - 1)
    def _():
        halo_copy().start()

    loads[0].wait()

    local = pos[0, 0] // 3 - t * tile_rows
    corner = jnp.clip(pos[0, 1] // 3 - n * tile_cols, 0, tile_cols - span)
    for w in range(win):
        row = local + w
        inside = (row >= 0) & (row < tile_rows)
        part = held[jnp.clip(row, 0, tile_rows - 1) + 1, pl.ds(PAD + corner, span)]
        band[w] = jnp.where(inside, part, 0.0)

    def gather_copy(g):
        return remote(
            band.at[:, pl.ds(g * LANES, LANES)], arrived.at[t], send1.at[g], recv1.at[t],
            relay0 + g, n,
        )

    for g in range(groups):
        @pl.when(t != relay0 + g)
        def _():
            gather_copy(g).start()

    edges[0] = held[1:tile_rows + 1, PAD]
    edges[1] = held[1:tile_rows + 1, PAD + tile_cols - 1]

    @pl.when(n < nn - 1)
    def _():
        right_copy().start()

    @pl.when(n > 0)
    def _():
        left_copy().start()

    for copy in loads[1:]:
        copy.wait()
    parent_operator = split_operator(pmix[...])

    def parent_rows(step, carry):
        half = tile_cols // 2
        for i in range(CHUNK):
            row = step * CHUNK + i
            for begin in (0, half):
                at = PAD + begin
                value = held[row + 1, at:at + half]
                around = (
                    held[row, at:at + half] + held[row + 2, at:at + half]
                    + held[row + 1, at + 1:at + 1 + half] + held[row + 1, at - 1:at - 1 + half]
                )
                fresh[row, begin:begin + half] = (
                    value + KAPPA * (around - 4.0 * value)
                    + apply_operator(value, parent_operator)
                )
        return carry

    chunks = tile_rows // CHUNK
    marks = [0, chunks // 2, chunks * 11 // 16, chunks * 14 // 16, chunks]
    lax.fori_loop(marks[0], marks[1], parent_rows, 0)

    is_relay = (t >= relay0) & (t < relay0 + groups)

    def spread_copy(r):
        return remote(
            reduced.at[pl.ds(low_row(r), count)], rows.at[t - relay0], send2.at[r],
            recv2.at[t - relay0], r, n,
        )

    def arrive_copy(s):
        return remote(
            band.at[:, pl.ds(0, LANES)], arrived.at[s], send1.at[0], recv1.at[s], s, n
        )

    for g in range(groups):
        @pl.when(t == relay0 + g)
        def _():
            reduced[...] = band[:, g * LANES:(g + 1) * LANES]

    for s in range(nt):
        @pl.when(is_relay & (t != s))
        def _():
            arrive_copy(s).wait_recv()
            reduced[...] += arrived[s]

    for r in range(nt):
        @pl.when(is_relay & (t != r))
        def _():
            spread_copy(r).start()

    for g in range(groups):
        @pl.when(t == relay0 + g)
        def _():
            rows[g] = reduced[pl.ds(low_row(t), count)]

    @pl.when(t < nt - 1)
    def _():
        down_copy().start()

    @pl.when(t > 0)
    def _():
        up_copy().start()

    lax.fori_loop(marks[1], marks[2], parent_rows, 0)

    operator = split_operator(nmix[...])
    shift_x = lax.rem(pos[0, 0], 3)
    shift_y = lax.rem(pos[0, 1], 3)
    span = (nest_cols, groups * LANES)
    table = hat(
        shift_y + lax.broadcasted_iota(jnp.int32, span, 0)
        - 3 * lax.broadcasted_iota(jnp.int32, span, 1)
    )
    first = t == 0

    @pl.when(t > 0)
    def _():
        halo_copy().wait_recv()

    for g in range(groups):
        @pl.when(t != relay0 + g)
        def _():
            remote(
                reduced.at[pl.ds(0, count)], rows.at[g], send2.at[0], recv2.at[g], t, n
            ).wait_recv()

    lines = [
        jnp.dot(
            table, rows[:, i].reshape(groups * LANES, width),
            precision=HIGH, preferred_element_type=jnp.float32,
        )
        for i in range(count)
    ]
    base = t * nest_rows
    lowest = low_row(t)
    total = nest_rows + STEPS
    for k in range(total):
        interp = None
        for i in range(count):
            weight = hat(shift_x + base - STEPS + k - 3 * (lowest + i))
            term = weight * lines[i]
            interp = term if interp is None else interp + term
        own = halo[k] if k < STEPS else state[k - STEPS]
        value = 0.5 * (own + interp)
        start[k] = value
        current[k] = value

    along_x = courant[0:1]
    along_y = courant[1:2]
    at_edge = lax.broadcasted_iota(jnp.int32, (nest_cols, width), 0) == 0
    for step in range(STEPS):
        for k in range(total - 1, step, -1):
            value = current[k]
            upper = current[k - 1]
            if k == STEPS:
                upper = jnp.where(first, start[k], upper)
            left = jnp.where(at_edge, start[k, 0:1], pltpu.roll(value, 1, 0))
            current[k] = (
                value + along_x * (upper - value) + along_y * (left - value)
                + apply_operator(value, operator)
            )

    lead_x = lax.rem(3 - lax.rem(shift_x + base, 3), 3)
    lead_y = lax.rem(3 - shift_y, 3)
    cells = feed.shape[2]
    pick = (
        lax.broadcasted_iota(jnp.int32, (cells, nest_cols), 1)
        == lead_y + 3 * lax.broadcasted_iota(jnp.int32, (cells, nest_cols), 0)
    ).astype(jnp.float32)
    r0, r1, r2, r3 = (current[STEPS + i] for i in range(nest_rows))
    chosen = jnp.where(lead_x == 0, r0, jnp.where(lead_x == 1, r1, r2))
    feed[t, 0] = jnp.dot(pick, chosen, precision=HIGH, preferred_element_type=jnp.float32)
    feed[t, 1] = jnp.dot(pick, r3, precision=HIGH, preferred_element_type=jnp.float32)

    hi_count = nt // lo_count
    hi, lo = t // lo_count, lax.rem(t, lo_count)

    def feed_copy(source, target, slot):
        return remote(feed.at[source], feed.at[source], send4.at[slot], recv4.at[source], target, n)

    sends = []
    for step in range(1, hi_count):
        sends.append(feed_copy(t, lax.rem(hi + step, hi_count) * lo_count + lo, len(sends)))
        sends[-1].start()
    for step in range(1, lo_count):
        sends.append(feed_copy(t, hi * lo_count + lax.rem(lo + step, lo_count), len(sends)))
        sends[-1].start()

    nest_out[...] = current[STEPS:]
    lax.fori_loop(marks[2], marks[3], parent_rows, 0)

    for step in range(1, hi_count):
        source = lax.rem(hi + step, hi_count) * lo_count + lo
        feed_copy(source, t, 0).wait_recv()
        for across in range(1, lo_count):
            target = hi * lo_count + lax.rem(lo + across, lo_count)
            sends.append(feed_copy(source, target, len(sends)))
            sends[-1].start()

    lax.fori_loop(marks[3], marks[4], parent_rows, 0)

    @pl.when(t > 0)
    def _():
        down_copy().wait_recv()

    @pl.when(t < nt - 1)
    def _():
        up_copy().wait_recv()

    @pl.when(n > 0)
    def _():
        right_copy().wait_recv()

    @pl.when(n < nn - 1)
    def _():
        left_copy().wait_recv()

    fresh[0] += KAPPA * above[...]
    fresh[tile_rows - 1] += KAPPA * below[...]
    fresh[:, 0] += KAPPA * beside[0]
    fresh[:, tile_cols - 1] += KAPPA * beside[1]
    out_copy = pltpu.make_async_copy(fresh, parent_new, store.at[0])
    out_copy.start()

    for across in range(1, lo_count):
        for step in range(hi_count):
            source = lax.rem(hi + step, hi_count) * lo_count + lax.rem(lo + across, lo_count)
            feed_copy(source, t, 0).wait_recv()

    for copy in sends:
        copy.wait_send()
    for g in range(groups):
        @pl.when(t != relay0 + g)
        def _():
            gather_copy(g).wait_send()
    for r in range(nt):
        @pl.when(is_relay & (t != r))
        def _():
            spread_copy(r).wait_send()

    @pl.when(t < nt - 1)
    def _():
        halo_copy().wait_send()
        down_copy().wait_send()

    @pl.when(t > 0)
    def _():
        up_copy().wait_send()

    @pl.when(n < nn - 1)
    def _():
        right_copy().wait_send()

    @pl.when(n > 0)
    def _():
        left_copy().wait_send()
    out_copy.wait()


def feedback_kernel(nest_rows, nest_total, nest_cols, pos, block, feed, nest, out, nest_out):
    step = pl.program_id(0)
    lines, cols, width = block.shape
    tile_rows = lines * pl.num_programs(0)

    @pl.when(step == 0)
    def _():
        nest_out[0] = nest[...]

    out[...] = block[...]
    lead_x = lax.rem(3 - lax.rem(pos[0, 0], 3), 3)
    lead_y = lax.rem(3 - lax.rem(pos[0, 1], 3), 3)
    top = (pos[0, 0] + lead_x) // 3 - lax.axis_index("tiles") * tile_rows
    first_col = (pos[0, 1] + lead_y) // 3 - lax.axis_index("nests") * cols
    cells = feed.shape[2]
    window = cells + 8
    base_col = pl.multiple_of(first_col // 8 * 8, 8)
    offset = first_col - base_col
    limit = (nest_cols - lead_y + 2) // 3
    for i in range(lines):
        x = lead_x + 3 * (step * lines + i - top)

        @pl.when((x >= 0) & (x < nest_total))
        def _():
            sender = x // nest_rows
            slot = (x - sender * nest_rows) // 3
            cell = lax.broadcasted_iota(jnp.int32, (window, width), 0) - offset
            fed = jnp.concatenate([feed[sender, slot], jnp.zeros((8, width), jnp.float32)], axis=0)
            fed = pltpu.roll(fed, offset, 0)
            old = out[i, pl.ds(base_col, window)]
            new = jnp.where((cell >= 0) & (cell < limit), old + 0.5 * (fed - old), old)
            out[i, pl.ds(base_col, window)] = new


def shards(nt, nn, parent, nest_state, parent_mix, nest_mix, courant, nest_pos):
    tile_rows, tile_cols, width = parent.shape
    _, nest_rows, nest_cols, _ = nest_state.shape
    nest_total = nest_rows * nt
    win = (nest_total + 1) // 3 + 2
    need = (nest_cols + 1) // 3 + 2
    span = -(-need // LANES) * LANES
    groups = span // LANES
    count = -(-(nest_rows + STEPS + 1) // 3) + 2
    fb_cols = -(-((nest_cols + 2) // 3) // LANES) * LANES
    lo_count = nt // 4
    slots = (nest_rows + 2) // 3
    vmem = pl.BlockSpec(memory_space=pltpu.VMEM)
    smem = pl.BlockSpec(memory_space=pltpu.SMEM)
    hbm = pl.BlockSpec(memory_space=pl.ANY)
    f32 = jnp.float32
    dma = pltpu.SemaphoreType.DMA
    nest_new, feed, parent_new = pl.pallas_call(
        functools.partial(exchange_kernel, nt, nn, lo_count),
        out_shape=(
            jax.ShapeDtypeStruct((nest_rows, nest_cols, width), f32),
            jax.ShapeDtypeStruct((nt, slots, fb_cols, width), f32),
            jax.ShapeDtypeStruct(parent.shape, f32),
        ),
        in_specs=[smem] + [hbm] * 5,
        out_specs=(vmem, vmem, hbm),
        scratch_shapes=[
            pltpu.VMEM((tile_rows + 2, tile_cols + 2 * PAD, width), f32),
            pltpu.VMEM((tile_rows, tile_cols, width), f32),
            pltpu.VMEM((win, span, width), f32),
            pltpu.VMEM((2, tile_rows, width), f32),
            pltpu.VMEM((tile_cols, width), f32),
            pltpu.VMEM((tile_cols, width), f32),
            pltpu.VMEM((2, tile_rows, width), f32),
            pltpu.VMEM((nest_rows, nest_cols, width), f32),
            pltpu.VMEM((width, width), f32),
            pltpu.VMEM((width, width), f32),
            pltpu.VMEM((2, width), f32),
            pltpu.VMEM((nt, win, LANES, width), f32),
            pltpu.VMEM((win, LANES, width), f32),
            pltpu.VMEM((groups, count, LANES, width), f32),
            pltpu.VMEM((STEPS, nest_cols, width), f32),
            pltpu.VMEM((nest_rows + STEPS, nest_cols, width), f32),
            pltpu.VMEM((nest_rows + STEPS, nest_cols, width), f32),
            dma((5,)), dma((1,)),
            dma((groups,)), dma((nt,)), dma((nt,)), dma((groups,)),
            dma((5,)), dma((5,)), dma((nt - 1,)), dma((nt,)),
        ],
        compiler_params=pltpu.CompilerParams(
            collective_id=0, has_side_effects=True, vmem_limit_bytes=VMEM_LIMIT
        ),
        name="nest_exchange",
    )(nest_pos, parent, nest_state, parent_mix, nest_mix, courant)

    lines = pl.BlockSpec((ROWS, tile_cols, width), lambda i: (i, 0, 0))
    return pl.pallas_call(
        functools.partial(feedback_kernel, nest_rows, nest_total, nest_cols),
        out_shape=(
            jax.ShapeDtypeStruct(parent.shape, f32),
            jax.ShapeDtypeStruct(nest_state.shape, f32),
        ),
        grid=(tile_rows // ROWS,),
        in_specs=[
            smem, lines,
            pl.BlockSpec(feed.shape, lambda i: (0, 0, 0, 0)),
            pl.BlockSpec(nest_new.shape, lambda i: (0, 0, 0)),
        ],
        out_specs=(lines, pl.BlockSpec(nest_state.shape, lambda i: (0, 0, 0, 0))),
        compiler_params=pltpu.CompilerParams(vmem_limit_bytes=VMEM_LIMIT),
        name="feedback",
    )(nest_pos, parent_new, feed, nest_new)


def solution(mesh):
    placed = (
        P("tiles", "nests", None),
        P("nests", "tiles", None, None),
        P(),
        P(),
        P(),
        P("nests", None),
    )
    return jax.shard_map(
        functools.partial(shards, mesh.shape["tiles"], mesh.shape["nests"]),
        mesh=mesh,
        in_specs=placed,
        out_specs=(P("tiles", "nests", None), P("nests", "tiles", None, None)),
        check_vma=False,
    )
```

```python
import functools

import jax
import jax.numpy as jnp
from jax import lax
from jax.experimental import pallas as pl
from jax.experimental.pallas import tpu as pltpu
from jax.sharding import PartitionSpec as P

STEPS = 3
KAPPA = 0.125
HIGH = lax.Precision.HIGHEST
MESH = pl.DeviceIdType.MESH
LANES = 8
CHUNK = 4
GROUP = 2
LOADS = 4
PAD = 8
VMEM_LIMIT = 40 * 1024 * 1024
FEED_LIMIT = 16 * 1024 * 1024


def split_operator(mix):
    high = mix.astype(jnp.bfloat16)
    low = (mix - high.astype(jnp.float32)).astype(jnp.bfloat16)
    upper = jnp.concatenate([high, low], axis=1)
    lower = jnp.concatenate([high, jnp.zeros_like(low)], axis=1)
    return jnp.concatenate([upper, lower], axis=0)


def apply_operator(values, operator):
    width = values.shape[-1]
    high = values.astype(jnp.bfloat16)
    low = (values - high.astype(jnp.float32)).astype(jnp.bfloat16)
    both = jnp.dot(
        jnp.concatenate([high, low], axis=1), operator, preferred_element_type=jnp.float32
    )
    return both[:, :width] + both[:, width:]


def hat(distance):
    return jnp.maximum(3 - jnp.abs(distance), 0).astype(jnp.float32) * (1.0 / 3.0)


def exchange_kernel(
    nt, nn, lo_count, pos, parent_hbm, state_hbm, pmix_hbm, nmix_hbm, courant_hbm,
    nest_out, feed, fresh,
    held, band, edges, above, below, beside, state, pmix, nmix, courant,
    arrived, reduced, rows, halo, current,
    load, send1, recv1, send2, recv2, send3, recv3, send4, recv4,
):
    t = lax.axis_index("tiles")
    n = lax.axis_index("nests")
    nest_rows, nest_cols, width = state.shape
    tile_rows, tile_cols, _ = fresh.shape
    win, span, _ = band.shape
    groups = span // LANES
    count = rows.shape[1]
    relay0 = (nt - groups) // 2

    def low_row(tile):
        return jnp.clip((tile * nest_rows - STEPS + 3) // 3 - 1, 0, win - count)

    def remote(src, dst, send, recv, tile, nest):
        return pltpu.make_async_remote_copy(
            src_ref=src, dst_ref=dst, send_sem=send, recv_sem=recv,
            device_id=(tile, nest), device_id_type=MESH,
        )

    share = tile_rows // LOADS
    parent_loads = [
        pltpu.make_async_copy(
            parent_hbm.at[pl.ds(i * share, share)],
            held.at[pl.ds(1 + i * share, share), pl.ds(PAD, tile_cols)], load.at[i],
        )
        for i in range(LOADS)
    ]
    small_loads = [
        pltpu.make_async_copy(pmix_hbm, pmix, load.at[LOADS]),
        pltpu.make_async_copy(state_hbm.at[0], state, load.at[LOADS + 1]),
        pltpu.make_async_copy(nmix_hbm, nmix, load.at[LOADS + 2]),
        pltpu.make_async_copy(courant_hbm, courant, load.at[LOADS + 3]),
    ]
    for copy in parent_loads + small_loads:
        copy.start()

    barrier = pltpu.get_barrier_semaphore()
    for step in range(1, nt):
        pl.semaphore_signal(
            barrier, inc=1, device_id=(lax.rem(t + step, nt), n), device_id_type=MESH
        )

    @pl.when(n > 0)
    def _():
        pl.semaphore_signal(barrier, inc=1, device_id=(t, n - 1), device_id_type=MESH)

    @pl.when(n < nn - 1)
    def _():
        pl.semaphore_signal(barrier, inc=1, device_id=(t, n + 1), device_id_type=MESH)

    held[0] = jnp.zeros(held.shape[1:], jnp.float32)
    held[tile_rows + 1] = jnp.zeros(held.shape[1:], jnp.float32)
    strip = jnp.zeros((tile_rows, PAD, width), jnp.float32)
    held[1:tile_rows + 1, :PAD] = strip
    held[1:tile_rows + 1, PAD + tile_cols:] = strip

    @pl.when(t == 0)
    def _():
        halo[...] = jnp.zeros_like(halo)
        above[...] = jnp.zeros_like(above)

    @pl.when(t == nt - 1)
    def _():
        below[...] = jnp.zeros_like(below)

    @pl.when(n == 0)
    def _():
        beside[0] = jnp.zeros(beside.shape[1:], jnp.float32)

    @pl.when(n == nn - 1)
    def _():
        beside[1] = jnp.zeros(beside.shape[1:], jnp.float32)

    peers = nt - 1 + (n > 0).astype(jnp.int32) + (n < nn - 1).astype(jnp.int32)
    pl.semaphore_wait(barrier, peers)

    def halo_copy():
        return remote(
            state_hbm.at[0, pl.ds(nest_rows - STEPS, STEPS)], halo, send3.at[0], recv3.at[0],
            t + 1, n,
        )

    def down_copy():
        return remote(
            parent_hbm.at[tile_rows - 1], above, send3.at[1], recv3.at[1], t + 1, n
        )

    def up_copy():
        return remote(parent_hbm.at[0], below, send3.at[2], recv3.at[2], t - 1, n)

    def right_copy():
        return remote(edges.at[1], beside.at[0], send3.at[3], recv3.at[3], t, n + 1)

    def left_copy():
        return remote(edges.at[0], beside.at[1], send3.at[4], recv3.at[4], t, n - 1)

    @pl.when(t < nt - 1)
    def _():
        halo_copy().start()

    for copy in parent_loads:
        copy.wait()

    local = pos[0, 0] // 3 - t * tile_rows
    corner = jnp.clip(pos[0, 1] // 3 - n * tile_cols, 0, tile_cols - span)
    for w in range(win):
        row = local + w
        inside = (row >= 0) & (row < tile_rows)
        part = held[jnp.clip(row, 0, tile_rows - 1) + 1, pl.ds(PAD + corner, span)]
        band[w] = jnp.where(inside, part, 0.0)

    def gather_copy(g):
        return remote(
            band.at[:, pl.ds(g * LANES, LANES)], arrived.at[t], send1.at[g], recv1.at[t],
            relay0 + g, n,
        )

    for g in range(groups):
        @pl.when(t != relay0 + g)
        def _():
            gather_copy(g).start()

    edges[0] = held[1:tile_rows + 1, PAD]
    edges[1] = held[1:tile_rows + 1, PAD + tile_cols - 1]

    @pl.when(n < nn - 1)
    def _():
        right_copy().start()

    @pl.when(n > 0)
    def _():
        left_copy().start()

    for copy in small_loads:
        copy.wait()
    parent_operator = split_operator(pmix[...])

    def parent_rows(step, carry):
        for i in range(0, CHUNK, GROUP):
            row = step * CHUNK + i
            value = held[pl.ds(row + 1, GROUP), PAD:PAD + tile_cols]
            around = (
                held[pl.ds(row, GROUP), PAD:PAD + tile_cols]
                + held[pl.ds(row + 2, GROUP), PAD:PAD + tile_cols]
                + held[pl.ds(row + 1, GROUP), PAD + 1:PAD + 1 + tile_cols]
                + held[pl.ds(row + 1, GROUP), PAD - 1:PAD - 1 + tile_cols]
            )
            mixed = apply_operator(value.reshape(GROUP * tile_cols, width), parent_operator)
            fresh[pl.ds(row, GROUP)] = (
                value + KAPPA * (around - 4.0 * value) + mixed.reshape(value.shape)
            )
        return carry

    chunks = tile_rows // CHUNK
    marks = [0, chunks // 2, chunks * 11 // 16, chunks * 14 // 16, chunks]
    lax.fori_loop(marks[0], marks[1], parent_rows, 0)

    is_relay = (t >= relay0) & (t < relay0 + groups)

    def spread_copy(r):
        return remote(
            reduced.at[pl.ds(low_row(r), count)], rows.at[t - relay0], send2.at[r],
            recv2.at[t - relay0], r, n,
        )

    def arrive_copy(s):
        return remote(
            band.at[:, pl.ds(0, LANES)], arrived.at[s], send1.at[0], recv1.at[s], s, n
        )

    for g in range(groups):
        @pl.when(t == relay0 + g)
        def _():
            reduced[...] = band[:, g * LANES:(g + 1) * LANES]

    for s in range(nt):
        @pl.when(is_relay & (t != s))
        def _():
            arrive_copy(s).wait_recv()
            reduced[...] += arrived[s]

    for r in range(nt):
        @pl.when(is_relay & (t != r))
        def _():
            spread_copy(r).start()

    for g in range(groups):
        @pl.when(t == relay0 + g)
        def _():
            rows[g] = reduced[pl.ds(low_row(t), count)]

    @pl.when(t < nt - 1)
    def _():
        down_copy().start()

    @pl.when(t > 0)
    def _():
        up_copy().start()

    lax.fori_loop(marks[1], marks[2], parent_rows, 0)

    operator = split_operator(nmix[...])
    shift_x = lax.rem(pos[0, 0], 3)
    shift_y = lax.rem(pos[0, 1], 3)
    span = (nest_cols, groups * LANES)
    table = hat(
        shift_y + lax.broadcasted_iota(jnp.int32, span, 0)
        - 3 * lax.broadcasted_iota(jnp.int32, span, 1)
    )
    first = t == 0

    @pl.when(t > 0)
    def _():
        halo_copy().wait_recv()

    for g in range(groups):
        @pl.when(t != relay0 + g)
        def _():
            remote(
                reduced.at[pl.ds(0, count)], rows.at[g], send2.at[0], recv2.at[g], t, n
            ).wait_recv()

    lines = [
        jnp.dot(
            table, rows[:, i].reshape(groups * LANES, width),
            precision=HIGH, preferred_element_type=jnp.float32,
        )
        for i in range(count)
    ]
    base = t * nest_rows
    lowest = low_row(t)
    total = nest_rows + STEPS
    for k in range(total):
        interp = None
        for i in range(count):
            weight = hat(shift_x + base - STEPS + k - 3 * (lowest + i))
            term = weight * lines[i]
            interp = term if interp is None else interp + term
        own = halo[k] if k < STEPS else state[k - STEPS]
        value = 0.5 * (own + interp)
        if k == STEPS:
            top = value
        current[k, PAD:] = value
        current[k, PAD - 1:PAD] = value[0:1]

    current[STEPS - 1, PAD:] = jnp.where(first, top, current[STEPS - 1, PAD:])
    along_x = courant[0:1]
    along_y = courant[1:2]
    for step in range(STEPS):
        value = current[step + 1:, PAD:]
        upper = current[step:total - 1, PAD:]
        left = current[step + 1:, PAD - 1:PAD - 1 + nest_cols]
        mixed = apply_operator(value.reshape(-1, width), operator).reshape(value.shape)
        value = value + along_x * (upper - value) + along_y * (left - value) + mixed
        current[step + 1:, PAD:] = value
        if step < STEPS - 1:
            current[STEPS - 1, PAD:] = jnp.where(first, top, value[STEPS - 2 - step])

    lead_x = lax.rem(3 - lax.rem(shift_x + base, 3), 3)
    lead_y = lax.rem(3 - shift_y, 3)
    cells = feed.shape[2]
    pick = (
        lax.broadcasted_iota(jnp.int32, (cells, nest_cols), 1)
        == lead_y + 3 * lax.broadcasted_iota(jnp.int32, (cells, nest_cols), 0)
    ).astype(jnp.float32)
    r0, r1, r2, r3 = (current[STEPS + i, PAD:] for i in range(nest_rows))
    chosen = jnp.where(lead_x == 0, r0, jnp.where(lead_x == 1, r1, r2))
    feed[t, 0] = jnp.dot(pick, chosen, precision=HIGH, preferred_element_type=jnp.float32)
    feed[t, 1] = jnp.dot(pick, r3, precision=HIGH, preferred_element_type=jnp.float32)

    hi_count = nt // lo_count
    hi, lo = t // lo_count, lax.rem(t, lo_count)

    def feed_copy(source, target, slot):
        return remote(feed.at[source], feed.at[source], send4.at[slot], recv4.at[source], target, n)

    sends = []
    for step in range(1, hi_count):
        sends.append(feed_copy(t, lax.rem(hi + step, hi_count) * lo_count + lo, len(sends)))
        sends[-1].start()
    for step in range(1, lo_count):
        sends.append(feed_copy(t, hi * lo_count + lax.rem(lo + step, lo_count), len(sends)))
        sends[-1].start()

    nest_out[...] = current[STEPS:, PAD:]
    lax.fori_loop(marks[2], marks[3], parent_rows, 0)

    for step in range(1, hi_count):
        source = lax.rem(hi + step, hi_count) * lo_count + lo
        feed_copy(source, t, 0).wait_recv()
        for across in range(1, lo_count):
            target = hi * lo_count + lax.rem(lo + across, lo_count)
            sends.append(feed_copy(source, target, len(sends)))
            sends[-1].start()

    lax.fori_loop(marks[3], marks[4], parent_rows, 0)

    @pl.when(t > 0)
    def _():
        down_copy().wait_recv()

    @pl.when(t < nt - 1)
    def _():
        up_copy().wait_recv()

    @pl.when(n > 0)
    def _():
        right_copy().wait_recv()

    @pl.when(n < nn - 1)
    def _():
        left_copy().wait_recv()

    fresh[0] += KAPPA * above[...]
    fresh[tile_rows - 1] += KAPPA * below[...]
    fresh[:, 0] += KAPPA * beside[0]
    fresh[:, tile_cols - 1] += KAPPA * beside[1]

    for across in range(1, lo_count):
        for step in range(hi_count):
            source = lax.rem(hi + step, hi_count) * lo_count + lax.rem(lo + across, lo_count)
            feed_copy(source, t, 0).wait_recv()

    for copy in sends:
        copy.wait_send()
    for g in range(groups):
        @pl.when(t != relay0 + g)
        def _():
            gather_copy(g).wait_send()
    for r in range(nt):
        @pl.when(is_relay & (t != r))
        def _():
            spread_copy(r).wait_send()

    @pl.when(t < nt - 1)
    def _():
        halo_copy().wait_send()
        down_copy().wait_send()

    @pl.when(t > 0)
    def _():
        up_copy().wait_send()

    @pl.when(n < nn - 1)
    def _():
        right_copy().wait_send()

    @pl.when(n > 0)
    def _():
        left_copy().wait_send()


def feedback_kernel(
    nest_rows, nest_total, nest_cols, pos, fresh, feed, nest, out, nest_out, patch, store, patched
):
    tile_rows, cols, width = fresh.shape
    share = tile_rows // LOADS
    copies = [
        pltpu.make_async_copy(
            fresh.at[pl.ds(i * share, share)], out.at[pl.ds(i * share, share)], store.at[i]
        )
        for i in range(LOADS)
    ]
    copies.append(pltpu.make_async_copy(nest, nest_out.at[0], store.at[LOADS]))
    for copy in copies:
        copy.start()
    lead_x = lax.rem(3 - lax.rem(pos[0, 0], 3), 3)
    lead_y = lax.rem(3 - lax.rem(pos[0, 1], 3), 3)
    top = (pos[0, 0] + lead_x) // 3 - lax.axis_index("tiles") * tile_rows
    first_col = (pos[0, 1] + lead_y) // 3 - lax.axis_index("nests") * cols
    window = patch.shape[1]
    base_col = pl.multiple_of(jnp.clip(first_col // 8 * 8, 0, cols - window), 8)
    offset = first_col - base_col
    limit = (nest_cols - lead_y + 2) // 3
    cell = lax.broadcasted_iota(jnp.int32, (window, width), 0) - offset
    live = (cell >= 0) & (cell < limit)

    def fed(k):
        return (lead_x + 3 * k < nest_total) & (top + k >= 0) & (top + k < tile_rows)

    def patch_copy(k):
        return pltpu.make_async_copy(
            patch.at[k], out.at[top + k, pl.ds(base_col, window)], patched.at[k]
        )

    for k in range(patch.shape[0]):
        @pl.when(fed(k))
        def _():
            x = lead_x + 3 * k
            sender = x // nest_rows
            slot = (x - sender * nest_rows) // 3
            values = jnp.concatenate(
                [feed[sender, slot], jnp.zeros((8, width), jnp.float32)], axis=0
            )
            values = pltpu.roll(values, offset, 0)
            old = fresh[top + k, pl.ds(base_col, window)]
            patch[k] = jnp.where(live, old + 0.5 * (values - old), old)

    for copy in copies:
        copy.wait()
    for k in range(patch.shape[0]):
        @pl.when(fed(k))
        def _():
            patch_copy(k).start()
    for k in range(patch.shape[0]):
        @pl.when(fed(k))
        def _():
            patch_copy(k).wait()


def shards(nt, nn, parent, nest_state, parent_mix, nest_mix, courant, nest_pos):
    tile_rows, tile_cols, width = parent.shape
    _, nest_rows, nest_cols, _ = nest_state.shape
    nest_total = nest_rows * nt
    win = (nest_total + 1) // 3 + 2
    need = (nest_cols + 1) // 3 + 2
    span = -(-need // LANES) * LANES
    groups = span // LANES
    count = -(-(nest_rows + STEPS + 1) // 3) + 2
    fb_cols = -(-((nest_cols + 2) // 3) // LANES) * LANES
    lo_count = nt // 4
    slots = (nest_rows + 2) // 3
    vmem = pl.BlockSpec(memory_space=pltpu.VMEM)
    smem = pl.BlockSpec(memory_space=pltpu.SMEM)
    hbm = pl.BlockSpec(memory_space=pltpu.HBM)
    f32 = jnp.float32
    dma = pltpu.SemaphoreType.DMA
    nest_pos, parent, nest_state, parent_mix, nest_mix, courant = (
        pltpu.with_memory_space_constraint(array, pltpu.HBM)
        for array in (nest_pos, parent, nest_state, parent_mix, nest_mix, courant)
    )
    nest_new, feed, parent_new = pl.pallas_call(
        functools.partial(exchange_kernel, nt, nn, lo_count),
        out_shape=(
            jax.ShapeDtypeStruct((nest_rows, nest_cols, width), f32),
            jax.ShapeDtypeStruct((nt, slots, fb_cols, width), f32),
            pltpu.VMEM(parent.shape, f32),
        ),
        in_specs=[smem] + [hbm] * 5,
        out_specs=(vmem, vmem, vmem),
        scratch_shapes=[
            pltpu.VMEM((tile_rows + 2, tile_cols + 2 * PAD, width), f32),
            pltpu.VMEM((win, span, width), f32),
            pltpu.VMEM((2, tile_rows, width), f32),
            pltpu.VMEM((tile_cols, width), f32),
            pltpu.VMEM((tile_cols, width), f32),
            pltpu.VMEM((2, tile_rows, width), f32),
            pltpu.VMEM((nest_rows, nest_cols, width), f32),
            pltpu.VMEM((width, width), f32),
            pltpu.VMEM((width, width), f32),
            pltpu.VMEM((2, width), f32),
            pltpu.VMEM((nt, win, LANES, width), f32),
            pltpu.VMEM((win, LANES, width), f32),
            pltpu.VMEM((groups, count, LANES, width), f32),
            pltpu.VMEM((STEPS, nest_cols, width), f32),
            pltpu.VMEM((nest_rows + STEPS, nest_cols + PAD, width), f32),
            dma((LOADS + 4,)),
            dma((groups,)), dma((nt,)), dma((nt,)), dma((groups,)),
            dma((5,)), dma((5,)), dma((nt - 1,)), dma((nt,)),
        ],
        compiler_params=pltpu.CompilerParams(
            collective_id=0, has_side_effects=True, vmem_limit_bytes=VMEM_LIMIT
        ),
        name="nest_exchange",
    )(nest_pos, parent, nest_state, parent_mix, nest_mix, courant)

    fed_rows = (nest_total + 2) // 3
    parent_new = pltpu.with_memory_space_constraint(parent_new, pltpu.VMEM)
    return pl.pallas_call(
        functools.partial(feedback_kernel, nest_rows, nest_total, nest_cols),
        out_shape=(
            jax.ShapeDtypeStruct(parent.shape, f32),
            jax.ShapeDtypeStruct(nest_state.shape, f32),
        ),
        in_specs=[smem, vmem, vmem, vmem],
        out_specs=(hbm, hbm),
        scratch_shapes=[
            pltpu.VMEM((fed_rows, fb_cols + 8, width), f32),
            dma((LOADS + 1,)), dma((fed_rows,)),
        ],
        compiler_params=pltpu.CompilerParams(vmem_limit_bytes=FEED_LIMIT),
        name="feedback",
    )(nest_pos, parent_new, feed, nest_new)


def solution(mesh):
    placed = (
        P("tiles", "nests", None),
        P("nests", "tiles", None, None),
        P(),
        P(),
        P(),
        P("nests", None),
    )
    return jax.shard_map(
        functools.partial(shards, mesh.shape["tiles"], mesh.shape["nests"]),
        mesh=mesh,
        in_specs=placed,
        out_specs=(P("tiles", "nests", None), P("nests", "tiles", None, None)),
        check_vma=False,
    )
```

```python
import functools

import jax
import jax.numpy as jnp
from jax import lax
from jax.experimental import pallas as pl
from jax.experimental.pallas import tpu as pltpu
from jax.sharding import PartitionSpec as P

STEPS = 3
KAPPA = 0.125
HIGH = lax.Precision.HIGHEST
MESH = pl.DeviceIdType.MESH
LANES = 8
CHUNK = 4
GROUP = 2
LOADS = 4
PAD = 8
VMEM_LIMIT = 40 * 1024 * 1024
FEED_LIMIT = 16 * 1024 * 1024


def split_operator(mix):
    high = mix.astype(jnp.bfloat16)
    low = (mix - high.astype(jnp.float32)).astype(jnp.bfloat16)
    upper = jnp.concatenate([high, low], axis=1)
    lower = jnp.concatenate([high, jnp.zeros_like(low)], axis=1)
    return jnp.concatenate([upper, lower], axis=0)


def apply_operator(values, operator):
    width = values.shape[-1]
    high = values.astype(jnp.bfloat16)
    low = (values - high.astype(jnp.float32)).astype(jnp.bfloat16)
    both = jnp.dot(
        jnp.concatenate([high, low], axis=1), operator, preferred_element_type=jnp.float32
    )
    return both[:, :width] + both[:, width:]


def hat(distance):
    return jnp.maximum(3 - jnp.abs(distance), 0).astype(jnp.float32) * (1.0 / 3.0)


def exchange_kernel(
    nt, nn, lo_count, pos, parent_hbm, state_hbm, pmix_hbm, nmix_hbm, courant_hbm,
    nest_out, feed, fresh,
    held, band, edges, above, below, beside, state, pmix, nmix, courant,
    arrived, reduced, rows, halo, current,
    load, send1, recv1, send2, recv2, send3, recv3, send4, recv4,
):
    t = lax.axis_index("tiles")
    n = lax.axis_index("nests")
    nest_rows, nest_cols, width = state.shape
    tile_rows, tile_cols, _ = fresh.shape
    win, span, _ = band.shape
    groups = span // LANES
    count = rows.shape[0]

    def low_row(tile):
        return (tile * nest_rows - STEPS + 3) // 3 - 1

    def cut(extent, parts, index):
        return extent * index // parts, extent * (index + 1) // parts

    lows = [min(max(low_row(tile), 0), win - count) for tile in range(nt)]
    parts = []
    for tile in range(nt):
        row_a, row_b = cut(win, nt // lo_count, tile // lo_count)
        col_a, col_b = cut(groups, lo_count, tile % lo_count)
        parts.append((row_a, row_b, col_a * LANES, col_b * LANES))

    def overlap(source, target):
        low = max(parts[source][0], lows[target])
        high = min(parts[source][1], lows[target] + count)
        return low, high

    def remote(src, dst, send, recv, tile, nest):
        return pltpu.make_async_remote_copy(
            src_ref=src, dst_ref=dst, send_sem=send, recv_sem=recv,
            device_id=(tile, nest), device_id_type=MESH,
        )

    share = tile_rows // LOADS
    parent_loads = [
        pltpu.make_async_copy(
            parent_hbm.at[pl.ds(i * share, share)],
            held.at[pl.ds(1 + i * share, share), pl.ds(PAD, tile_cols)], load.at[i],
        )
        for i in range(LOADS)
    ]
    small_loads = [
        pltpu.make_async_copy(pmix_hbm, pmix, load.at[LOADS]),
        pltpu.make_async_copy(state_hbm.at[0], state, load.at[LOADS + 1]),
        pltpu.make_async_copy(nmix_hbm, nmix, load.at[LOADS + 2]),
        pltpu.make_async_copy(courant_hbm, courant, load.at[LOADS + 3]),
    ]
    for copy in parent_loads + small_loads:
        copy.start()

    barrier = pltpu.get_barrier_semaphore()
    for step in range(1, nt):
        pl.semaphore_signal(
            barrier, inc=1, device_id=(lax.rem(t + step, nt), n), device_id_type=MESH
        )

    @pl.when(n > 0)
    def _():
        pl.semaphore_signal(barrier, inc=1, device_id=(t, n - 1), device_id_type=MESH)

    @pl.when(n < nn - 1)
    def _():
        pl.semaphore_signal(barrier, inc=1, device_id=(t, n + 1), device_id_type=MESH)

    held[0] = jnp.zeros(held.shape[1:], jnp.float32)
    held[tile_rows + 1] = jnp.zeros(held.shape[1:], jnp.float32)
    strip = jnp.zeros((tile_rows, PAD, width), jnp.float32)
    held[1:tile_rows + 1, :PAD] = strip
    held[1:tile_rows + 1, PAD + tile_cols:] = strip

    @pl.when(t == 0)
    def _():
        halo[...] = jnp.zeros_like(halo)
        above[...] = jnp.zeros_like(above)

    @pl.when(t == nt - 1)
    def _():
        below[...] = jnp.zeros_like(below)

    @pl.when(n == 0)
    def _():
        beside[0] = jnp.zeros(beside.shape[1:], jnp.float32)

    @pl.when(n == nn - 1)
    def _():
        beside[1] = jnp.zeros(beside.shape[1:], jnp.float32)

    peers = nt - 1 + (n > 0).astype(jnp.int32) + (n < nn - 1).astype(jnp.int32)
    pl.semaphore_wait(barrier, peers)

    def halo_copy():
        return remote(
            state_hbm.at[0, pl.ds(nest_rows - STEPS, STEPS)], halo, send3.at[0], recv3.at[0],
            t + 1, n,
        )

    def down_copy():
        return remote(
            parent_hbm.at[tile_rows - 1], above, send3.at[1], recv3.at[1], t + 1, n
        )

    def up_copy():
        return remote(parent_hbm.at[0], below, send3.at[2], recv3.at[2], t - 1, n)

    def right_copy():
        return remote(edges.at[1], beside.at[0], send3.at[3], recv3.at[3], t, n + 1)

    def left_copy():
        return remote(edges.at[0], beside.at[1], send3.at[4], recv3.at[4], t, n - 1)

    @pl.when(t < nt - 1)
    def _():
        halo_copy().start()

    for copy in parent_loads:
        copy.wait()

    local = pos[0, 0] // 3 - t * tile_rows
    corner = jnp.clip(pos[0, 1] // 3 - n * tile_cols, 0, tile_cols - span)
    for w in range(win):
        row = local + w
        inside = (row >= 0) & (row < tile_rows)
        part = held[jnp.clip(row, 0, tile_rows - 1) + 1, pl.ds(PAD + corner, span)]
        band[w] = jnp.where(inside, part, 0.0)

    def gather_copy(source, target):
        row_a, row_b, col_a, col_b = parts[target]
        return remote(
            band.at[row_a:row_b, col_a:col_b],
            arrived.at[source, 0:row_b - row_a, 0:col_b - col_a],
            send1.at[target], recv1.at[source], target, n,
        )

    for r in range(nt):
        @pl.when(t != r)
        def _():
            gather_copy(t, r).start()

    edges[0] = held[1:tile_rows + 1, PAD]
    edges[1] = held[1:tile_rows + 1, PAD + tile_cols - 1]

    @pl.when(n < nn - 1)
    def _():
        right_copy().start()

    @pl.when(n > 0)
    def _():
        left_copy().start()

    for copy in small_loads:
        copy.wait()
    parent_operator = split_operator(pmix[...])

    def parent_rows(step, carry):
        for i in range(0, CHUNK, GROUP):
            row = step * CHUNK + i
            value = held[pl.ds(row + 1, GROUP), PAD:PAD + tile_cols]
            around = (
                held[pl.ds(row, GROUP), PAD:PAD + tile_cols]
                + held[pl.ds(row + 2, GROUP), PAD:PAD + tile_cols]
                + held[pl.ds(row + 1, GROUP), PAD + 1:PAD + 1 + tile_cols]
                + held[pl.ds(row + 1, GROUP), PAD - 1:PAD - 1 + tile_cols]
            )
            mixed = apply_operator(value.reshape(GROUP * tile_cols, width), parent_operator)
            fresh[pl.ds(row, GROUP)] = (
                value + KAPPA * (around - 4.0 * value) + mixed.reshape(value.shape)
            )
        return carry

    chunks = tile_rows // CHUNK
    marks = [0, chunks * 9 // 16, chunks * 12 // 16, chunks * 14 // 16, chunks]
    lax.fori_loop(marks[0], marks[1], parent_rows, 0)

    def spread_copy(source, target):
        row_a, _, col_a, col_b = parts[source]
        low, high = overlap(source, target)
        return remote(
            reduced.at[low - row_a:high - row_a, 0:col_b - col_a],
            rows.at[low - lows[target]:high - lows[target], col_a:col_b],
            send2.at[target], recv2.at[source], target, n,
        )

    def needs(source, target):
        low, high = overlap(source, target)
        return low < high and parts[source][2] < parts[source][3]

    for r in range(nt):
        row_a, row_b, col_a, col_b = parts[r]

        @pl.when(t == r)
        def _():
            total = band[row_a:row_b, col_a:col_b]
            for s in range(nt):
                if s != r:
                    gather_copy(s, r).wait_recv()
                    total = total + arrived[s, 0:row_b - row_a, 0:col_b - col_a]
            reduced[0:row_b - row_a, 0:col_b - col_a] = total
            for q in range(nt):
                if q != r and needs(r, q):
                    spread_copy(r, q).start()
            low, high = overlap(r, r)
            if needs(r, r):
                rows[low - lows[r]:high - lows[r], col_a:col_b] = (
                    reduced[low - row_a:high - row_a, 0:col_b - col_a]
                )

    @pl.when(t < nt - 1)
    def _():
        down_copy().start()

    @pl.when(t > 0)
    def _():
        up_copy().start()

    lax.fori_loop(marks[1], marks[2], parent_rows, 0)

    operator = split_operator(nmix[...])
    shift_x = lax.rem(pos[0, 0], 3)
    shift_y = lax.rem(pos[0, 1], 3)
    span = (nest_cols, groups * LANES)
    table = hat(
        shift_y + lax.broadcasted_iota(jnp.int32, span, 0)
        - 3 * lax.broadcasted_iota(jnp.int32, span, 1)
    )
    first = t == 0

    @pl.when(t > 0)
    def _():
        halo_copy().wait_recv()

    for q in range(nt):
        @pl.when(t == q)
        def _():
            for r in range(nt):
                if r != q and needs(r, q):
                    spread_copy(r, q).wait_recv()

    lines = [
        jnp.dot(
            table, rows[i],
            precision=HIGH, preferred_element_type=jnp.float32,
        )
        for i in range(count)
    ]
    base = t * nest_rows
    lowest = jnp.clip(low_row(t), 0, win - count)
    total = nest_rows + STEPS
    for k in range(total):
        interp = None
        for i in range(count):
            weight = hat(shift_x + base - STEPS + k - 3 * (lowest + i))
            term = weight * lines[i]
            interp = term if interp is None else interp + term
        own = halo[k] if k < STEPS else state[k - STEPS]
        value = 0.5 * (own + interp)
        if k == STEPS:
            top = value
        current[k, PAD:] = value
        current[k, PAD - 1:PAD] = value[0:1]

    current[STEPS - 1, PAD:] = jnp.where(first, top, current[STEPS - 1, PAD:])
    along_x = courant[0:1]
    along_y = courant[1:2]
    for step in range(STEPS):
        value = current[step + 1:, PAD:]
        upper = current[step:total - 1, PAD:]
        left = current[step + 1:, PAD - 1:PAD - 1 + nest_cols]
        mixed = apply_operator(value.reshape(-1, width), operator).reshape(value.shape)
        value = value + along_x * (upper - value) + along_y * (left - value) + mixed
        current[step + 1:, PAD:] = value
        if step < STEPS - 1:
            current[STEPS - 1, PAD:] = jnp.where(first, top, value[STEPS - 2 - step])

    lead_x = lax.rem(3 - lax.rem(shift_x + base, 3), 3)
    lead_y = lax.rem(3 - shift_y, 3)
    cells = feed.shape[2]
    pick = (
        lax.broadcasted_iota(jnp.int32, (cells, nest_cols), 1)
        == lead_y + 3 * lax.broadcasted_iota(jnp.int32, (cells, nest_cols), 0)
    ).astype(jnp.float32)
    r0, r1, r2, r3 = (current[STEPS + i, PAD:] for i in range(nest_rows))
    chosen = jnp.where(lead_x == 0, r0, jnp.where(lead_x == 1, r1, r2))
    feed[t, 0] = jnp.dot(pick, chosen, precision=HIGH, preferred_element_type=jnp.float32)
    feed[t, 1] = jnp.dot(pick, r3, precision=HIGH, preferred_element_type=jnp.float32)

    hi_count = nt // lo_count
    hi, lo = t // lo_count, lax.rem(t, lo_count)

    def feed_copy(source, target, slot):
        return remote(feed.at[source], feed.at[source], send4.at[slot], recv4.at[source], target, n)

    sends = []
    for step in range(1, hi_count):
        sends.append(feed_copy(t, lax.rem(hi + step, hi_count) * lo_count + lo, len(sends)))
        sends[-1].start()
    for step in range(1, lo_count):
        sends.append(feed_copy(t, hi * lo_count + lax.rem(lo + step, lo_count), len(sends)))
        sends[-1].start()

    nest_out[...] = current[STEPS:, PAD:]
    lax.fori_loop(marks[2], marks[3], parent_rows, 0)

    for step in range(1, hi_count):
        source = lax.rem(hi + step, hi_count) * lo_count + lo
        feed_copy(source, t, 0).wait_recv()
        for across in range(1, lo_count):
            target = hi * lo_count + lax.rem(lo + across, lo_count)
            sends.append(feed_copy(source, target, len(sends)))
            sends[-1].start()

    lax.fori_loop(marks[3], marks[4], parent_rows, 0)

    @pl.when(t > 0)
    def _():
        down_copy().wait_recv()

    @pl.when(t < nt - 1)
    def _():
        up_copy().wait_recv()

    @pl.when(n > 0)
    def _():
        right_copy().wait_recv()

    @pl.when(n < nn - 1)
    def _():
        left_copy().wait_recv()

    fresh[0] += KAPPA * above[...]
    fresh[tile_rows - 1] += KAPPA * below[...]
    fresh[:, 0] += KAPPA * beside[0]
    fresh[:, tile_cols - 1] += KAPPA * beside[1]

    for across in range(1, lo_count):
        for step in range(hi_count):
            source = lax.rem(hi + step, hi_count) * lo_count + lax.rem(lo + across, lo_count)
            feed_copy(source, t, 0).wait_recv()

    for copy in sends:
        copy.wait_send()
    for r in range(nt):
        @pl.when(t != r)
        def _():
            gather_copy(t, r).wait_send()

        @pl.when(t == r)
        def _():
            for q in range(nt):
                if q != r and needs(r, q):
                    spread_copy(r, q).wait_send()

    @pl.when(t < nt - 1)
    def _():
        halo_copy().wait_send()
        down_copy().wait_send()

    @pl.when(t > 0)
    def _():
        up_copy().wait_send()

    @pl.when(n < nn - 1)
    def _():
        right_copy().wait_send()

    @pl.when(n > 0)
    def _():
        left_copy().wait_send()


def feedback_kernel(
    nest_rows, nest_total, nest_cols, pos, fresh, feed, nest, out, nest_out, patch, store, patched
):
    tile_rows, cols, width = fresh.shape
    share = tile_rows // LOADS
    copies = [
        pltpu.make_async_copy(
            fresh.at[pl.ds(i * share, share)], out.at[pl.ds(i * share, share)], store.at[i]
        )
        for i in range(LOADS)
    ]
    copies.append(pltpu.make_async_copy(nest, nest_out.at[0], store.at[LOADS]))
    for copy in copies:
        copy.start()
    lead_x = lax.rem(3 - lax.rem(pos[0, 0], 3), 3)
    lead_y = lax.rem(3 - lax.rem(pos[0, 1], 3), 3)
    top = (pos[0, 0] + lead_x) // 3 - lax.axis_index("tiles") * tile_rows
    first_col = (pos[0, 1] + lead_y) // 3 - lax.axis_index("nests") * cols
    window = patch.shape[1]
    base_col = pl.multiple_of(jnp.clip(first_col // 8 * 8, 0, cols - window), 8)
    offset = first_col - base_col
    limit = (nest_cols - lead_y + 2) // 3
    cell = lax.broadcasted_iota(jnp.int32, (window, width), 0) - offset
    live = (cell >= 0) & (cell < limit)

    def fed(k):
        return (lead_x + 3 * k < nest_total) & (top + k >= 0) & (top + k < tile_rows)

    def patch_copy(k):
        return pltpu.make_async_copy(
            patch.at[k], out.at[top + k, pl.ds(base_col, window)], patched.at[k]
        )

    for k in range(patch.shape[0]):
        @pl.when(fed(k))
        def _():
            x = lead_x + 3 * k
            sender = x // nest_rows
            slot = (x - sender * nest_rows) // 3
            values = jnp.concatenate(
                [feed[sender, slot], jnp.zeros((8, width), jnp.float32)], axis=0
            )
            values = pltpu.roll(values, offset, 0)
            old = fresh[top + k, pl.ds(base_col, window)]
            patch[k] = jnp.where(live, old + 0.5 * (values - old), old)

    for copy in copies:
        copy.wait()
    for k in range(patch.shape[0]):
        @pl.when(fed(k))
        def _():
            patch_copy(k).start()
    for k in range(patch.shape[0]):
        @pl.when(fed(k))
        def _():
            patch_copy(k).wait()


def shards(nt, nn, parent, nest_state, parent_mix, nest_mix, courant, nest_pos):
    tile_rows, tile_cols, width = parent.shape
    _, nest_rows, nest_cols, _ = nest_state.shape
    nest_total = nest_rows * nt
    win = (nest_total + 1) // 3 + 2
    need = (nest_cols + 1) // 3 + 2
    span = -(-need // LANES) * LANES
    groups = span // LANES
    count = -(-(nest_rows + STEPS + 1) // 3) + 2
    fb_cols = -(-((nest_cols + 2) // 3) // LANES) * LANES
    lo_count = nt // 4
    slots = (nest_rows + 2) // 3
    part_rows = -(-win // (nt // lo_count))
    part_cols = -(-groups // lo_count) * LANES
    vmem = pl.BlockSpec(memory_space=pltpu.VMEM)
    smem = pl.BlockSpec(memory_space=pltpu.SMEM)
    hbm = pl.BlockSpec(memory_space=pltpu.HBM)
    f32 = jnp.float32
    dma = pltpu.SemaphoreType.DMA
    nest_pos, parent, nest_state, parent_mix, nest_mix, courant = (
        pltpu.with_memory_space_constraint(array, pltpu.HBM)
        for array in (nest_pos, parent, nest_state, parent_mix, nest_mix, courant)
    )
    nest_new, feed, parent_new = pl.pallas_call(
        functools.partial(exchange_kernel, nt, nn, lo_count),
        out_shape=(
            jax.ShapeDtypeStruct((nest_rows, nest_cols, width), f32),
            jax.ShapeDtypeStruct((nt, slots, fb_cols, width), f32),
            pltpu.VMEM(parent.shape, f32),
        ),
        in_specs=[smem] + [hbm] * 5,
        out_specs=(vmem, vmem, vmem),
        scratch_shapes=[
            pltpu.VMEM((tile_rows + 2, tile_cols + 2 * PAD, width), f32),
            pltpu.VMEM((win, span, width), f32),
            pltpu.VMEM((2, tile_rows, width), f32),
            pltpu.VMEM((tile_cols, width), f32),
            pltpu.VMEM((tile_cols, width), f32),
            pltpu.VMEM((2, tile_rows, width), f32),
            pltpu.VMEM((nest_rows, nest_cols, width), f32),
            pltpu.VMEM((width, width), f32),
            pltpu.VMEM((width, width), f32),
            pltpu.VMEM((2, width), f32),
            pltpu.VMEM((nt, part_rows, part_cols, width), f32),
            pltpu.VMEM((part_rows, part_cols, width), f32),
            pltpu.VMEM((count, span, width), f32),
            pltpu.VMEM((STEPS, nest_cols, width), f32),
            pltpu.VMEM((nest_rows + STEPS, nest_cols + PAD, width), f32),
            dma((LOADS + 4,)),
            dma((nt,)), dma((nt,)), dma((nt,)), dma((nt,)),
            dma((5,)), dma((5,)), dma((nt - 1,)), dma((nt,)),
        ],
        compiler_params=pltpu.CompilerParams(
            collective_id=0, has_side_effects=True, vmem_limit_bytes=VMEM_LIMIT
        ),
        name="nest_exchange",
    )(nest_pos, parent, nest_state, parent_mix, nest_mix, courant)

    fed_rows = (nest_total + 2) // 3
    parent_new = pltpu.with_memory_space_constraint(parent_new, pltpu.VMEM)
    return pl.pallas_call(
        functools.partial(feedback_kernel, nest_rows, nest_total, nest_cols),
        out_shape=(
            jax.ShapeDtypeStruct(parent.shape, f32),
            jax.ShapeDtypeStruct(nest_state.shape, f32),
        ),
        in_specs=[smem, vmem, vmem, vmem],
        out_specs=(hbm, hbm),
        scratch_shapes=[
            pltpu.VMEM((fed_rows, fb_cols + 8, width), f32),
            dma((LOADS + 1,)), dma((fed_rows,)),
        ],
        compiler_params=pltpu.CompilerParams(vmem_limit_bytes=FEED_LIMIT),
        name="feedback",
    )(nest_pos, parent_new, feed, nest_new)


def solution(mesh):
    placed = (
        P("tiles", "nests", None),
        P("nests", "tiles", None, None),
        P(),
        P(),
        P(),
        P("nests", None),
    )
    return jax.shard_map(
        functools.partial(shards, mesh.shape["tiles"], mesh.shape["nests"]),
        mesh=mesh,
        in_specs=placed,
        out_specs=(P("tiles", "nests", None), P("nests", "tiles", None, None)),
        check_vma=False,
    )
```

```python
import functools

import jax
import jax.numpy as jnp
from jax import lax
from jax.experimental import pallas as pl
from jax.experimental.pallas import tpu as pltpu
from jax.sharding import PartitionSpec as P

STEPS = 3
KAPPA = 0.125
HIGH = lax.Precision.HIGHEST
MESH = pl.DeviceIdType.MESH
LANES = 8
CHUNK = 4
GROUP = 2
LOADS = 4
PAD = 8
VMEM_LIMIT = 40 * 1024 * 1024
FEED_LIMIT = 16 * 1024 * 1024


def split_operator(mix):
    high = mix.astype(jnp.bfloat16)
    low = (mix - high.astype(jnp.float32)).astype(jnp.bfloat16)
    upper = jnp.concatenate([high, low], axis=1)
    lower = jnp.concatenate([high, jnp.zeros_like(low)], axis=1)
    return jnp.concatenate([upper, lower], axis=0)


def apply_operator(values, operator):
    width = values.shape[-1]
    high = values.astype(jnp.bfloat16)
    low = (values - high.astype(jnp.float32)).astype(jnp.bfloat16)
    both = jnp.dot(
        jnp.concatenate([high, low], axis=1), operator, preferred_element_type=jnp.float32
    )
    return both[:, :width] + both[:, width:]


def hat(distance):
    return jnp.maximum(3 - jnp.abs(distance), 0).astype(jnp.float32) * (1.0 / 3.0)


def exchange_kernel(
    nt, nn, lo_count, pos, parent_hbm, state_hbm, pmix_hbm, nmix_hbm, courant_hbm,
    nest_out, feed, fresh,
    held, band, edges, above, below, beside, state, pmix, nmix, courant,
    early, mine, arrived, reduced, rows, halo, current,
    load, send0, recv0, send1, recv1, send2, recv2, send3, recv3, send4, recv4,
):
    t = lax.axis_index("tiles")
    n = lax.axis_index("nests")
    nest_rows, nest_cols, width = state.shape
    tile_rows, tile_cols, _ = fresh.shape
    win, span, _ = band.shape
    groups = span // LANES
    count = rows.shape[0]

    def low_row(tile):
        return (tile * nest_rows - STEPS + 3) // 3 - 1

    def cut(extent, parts, index):
        return extent * index // parts, extent * (index + 1) // parts

    lows = [min(max(low_row(tile), 0), win - count) for tile in range(nt)]
    parts = []
    for tile in range(nt):
        row_a, row_b = cut(win, nt // lo_count, tile // lo_count)
        col_a, col_b = cut(groups, lo_count, tile % lo_count)
        parts.append((row_a, row_b, col_a * LANES, col_b * LANES))

    def overlap(source, target):
        low = max(parts[source][0], lows[target])
        high = min(parts[source][1], lows[target] + count)
        return low, high

    def remote(src, dst, send, recv, tile, nest):
        return pltpu.make_async_remote_copy(
            src_ref=src, dst_ref=dst, send_sem=send, recv_sem=recv,
            device_id=(tile, nest), device_id_type=MESH,
        )

    share = tile_rows // LOADS
    parent_loads = [
        pltpu.make_async_copy(
            parent_hbm.at[pl.ds(i * share, share)],
            held.at[pl.ds(1 + i * share, share), pl.ds(PAD, tile_cols)], load.at[i],
        )
        for i in range(LOADS)
    ]
    small_loads = [
        pltpu.make_async_copy(pmix_hbm, pmix, load.at[LOADS]),
        pltpu.make_async_copy(state_hbm.at[0], state, load.at[LOADS + 1]),
        pltpu.make_async_copy(nmix_hbm, nmix, load.at[LOADS + 2]),
        pltpu.make_async_copy(courant_hbm, courant, load.at[LOADS + 3]),
    ]
    for copy in parent_loads + small_loads:
        copy.start()

    barrier = pltpu.get_barrier_semaphore()
    for step in range(1, nt):
        pl.semaphore_signal(
            barrier, inc=1, device_id=(lax.rem(t + step, nt), n), device_id_type=MESH
        )

    @pl.when(n > 0)
    def _():
        pl.semaphore_signal(barrier, inc=1, device_id=(t, n - 1), device_id_type=MESH)

    @pl.when(n < nn - 1)
    def _():
        pl.semaphore_signal(barrier, inc=1, device_id=(t, n + 1), device_id_type=MESH)

    held[0] = jnp.zeros(held.shape[1:], jnp.float32)
    held[tile_rows + 1] = jnp.zeros(held.shape[1:], jnp.float32)
    strip = jnp.zeros((tile_rows, PAD, width), jnp.float32)
    held[1:tile_rows + 1, :PAD] = strip
    held[1:tile_rows + 1, PAD + tile_cols:] = strip

    @pl.when(t == 0)
    def _():
        halo[...] = jnp.zeros_like(halo)
        above[...] = jnp.zeros_like(above)

    @pl.when(t == nt - 1)
    def _():
        below[...] = jnp.zeros_like(below)

    @pl.when(n == 0)
    def _():
        beside[0] = jnp.zeros(beside.shape[1:], jnp.float32)

    @pl.when(n == nn - 1)
    def _():
        beside[1] = jnp.zeros(beside.shape[1:], jnp.float32)

    peers = nt - 1 + (n > 0).astype(jnp.int32) + (n < nn - 1).astype(jnp.int32)
    pl.semaphore_wait(barrier, peers)

    def halo_copy():
        return remote(
            state_hbm.at[0, pl.ds(nest_rows - STEPS, STEPS)], halo, send3.at[0], recv3.at[0],
            t + 1, n,
        )

    def down_copy():
        return remote(
            parent_hbm.at[tile_rows - 1], above, send3.at[1], recv3.at[1], t + 1, n
        )

    def up_copy():
        return remote(parent_hbm.at[0], below, send3.at[2], recv3.at[2], t - 1, n)

    def right_copy():
        return remote(edges.at[1], beside.at[0], send3.at[3], recv3.at[3], t, n + 1)

    def left_copy():
        return remote(edges.at[0], beside.at[1], send3.at[4], recv3.at[4], t, n - 1)

    @pl.when(t < nt - 1)
    def _():
        halo_copy().start()

    @pl.when(t > 0)
    def _():
        up_copy().start()

    for copy in parent_loads:
        copy.wait()

    local = pos[0, 0] // 3 - t * tile_rows
    corner = jnp.clip(pos[0, 1] // 3 - n * tile_cols, 0, tile_cols - span)
    for w in range(win):
        row = local + w
        inside = (row >= 0) & (row < tile_rows)
        part = held[jnp.clip(row, 0, tile_rows - 1) + 1, pl.ds(PAD + corner, span)]
        band[w] = jnp.where(inside, part, 0.0)

    hi_count = nt // lo_count

    def chunk_order(tile):
        return sorted(range(hi_count), key=lambda h: -abs(h - tile // lo_count))

    def early_copy(source, target, chunk):
        row_a, row_b, col_a, col_b = parts[chunk * lo_count + target % lo_count]
        return remote(
            band.at[row_a:row_b, col_a:col_b],
            early.at[source % lo_count, row_a:row_b, 0:col_b - col_a],
            send0.at[target % lo_count, chunk], recv0.at[source % lo_count, chunk], target, n,
        )

    def gather_copy(source, target):
        row_a, row_b, col_a, col_b = parts[target]
        return remote(
            mine.at[row_a:row_b, 0:col_b - col_a],
            arrived.at[source // lo_count, 0:row_b - row_a, 0:col_b - col_a],
            send1.at[target // lo_count], recv1.at[source // lo_count], target, n,
        )

    def same_hi(tile):
        first_one = tile // lo_count * lo_count
        return [other for other in range(first_one, first_one + lo_count) if other != tile]

    def same_lo(tile):
        return [other for other in range(tile % lo_count, nt, lo_count) if other != tile]

    for r in range(nt):
        @pl.when(t == r)
        def _():
            for chunk in chunk_order(r):
                for other in same_hi(r):
                    early_copy(r, other, chunk).start()

    edges[0] = held[1:tile_rows + 1, PAD]
    edges[1] = held[1:tile_rows + 1, PAD + tile_cols - 1]

    @pl.when(n < nn - 1)
    def _():
        right_copy().start()

    @pl.when(n > 0)
    def _():
        left_copy().start()

    for copy in small_loads:
        copy.wait()
    parent_operator = split_operator(pmix[...])

    def parent_rows(step, carry):
        for i in range(0, CHUNK, GROUP):
            row = step * CHUNK + i
            value = held[pl.ds(row + 1, GROUP), PAD:PAD + tile_cols]
            around = (
                held[pl.ds(row, GROUP), PAD:PAD + tile_cols]
                + held[pl.ds(row + 2, GROUP), PAD:PAD + tile_cols]
                + held[pl.ds(row + 1, GROUP), PAD + 1:PAD + 1 + tile_cols]
                + held[pl.ds(row + 1, GROUP), PAD - 1:PAD - 1 + tile_cols]
            )
            mixed = apply_operator(value.reshape(GROUP * tile_cols, width), parent_operator)
            fresh[pl.ds(row, GROUP)] = (
                value + KAPPA * (around - 4.0 * value) + mixed.reshape(value.shape)
            )
        return carry

    chunks = tile_rows // CHUNK
    marks = [chunks * m // 16 for m in (0, 2, 9, 12, 14, 16)]
    lax.fori_loop(marks[0], marks[1], parent_rows, 0)

    for r in range(nt):
        @pl.when(t == r)
        def _():
            for chunk in chunk_order(r):
                row_a, row_b, col_a, col_b = parts[chunk * lo_count + r % lo_count]
                total = band[row_a:row_b, col_a:col_b]
                for other in same_hi(r):
                    early_copy(other, r, chunk).wait_recv()
                    total = total + early[other % lo_count, row_a:row_b, 0:col_b - col_a]
                mine[row_a:row_b, 0:col_b - col_a] = total
                if chunk != r // lo_count:
                    gather_copy(r, chunk * lo_count + r % lo_count).start()

    lax.fori_loop(marks[1], marks[2], parent_rows, 0)

    def spread_copy(source, target):
        row_a, _, col_a, col_b = parts[source]
        low, high = overlap(source, target)
        return remote(
            reduced.at[low - row_a:high - row_a, 0:col_b - col_a],
            rows.at[low - lows[target]:high - lows[target], col_a:col_b],
            send2.at[target], recv2.at[source], target, n,
        )

    def needs(source, target):
        low, high = overlap(source, target)
        return low < high and parts[source][2] < parts[source][3]

    for r in range(nt):
        row_a, row_b, col_a, col_b = parts[r]

        @pl.when(t == r)
        def _():
            total = mine[row_a:row_b, 0:col_b - col_a]
            for s in same_lo(r):
                gather_copy(s, r).wait_recv()
                total = total + arrived[s // lo_count, 0:row_b - row_a, 0:col_b - col_a]
            reduced[0:row_b - row_a, 0:col_b - col_a] = total
            for q in range(nt):
                if q != r and needs(r, q):
                    spread_copy(r, q).start()
            low, high = overlap(r, r)
            if needs(r, r):
                rows[low - lows[r]:high - lows[r], col_a:col_b] = (
                    reduced[low - row_a:high - row_a, 0:col_b - col_a]
                )

    @pl.when(t < nt - 1)
    def _():
        down_copy().start()

    lax.fori_loop(marks[2], marks[3], parent_rows, 0)

    operator = split_operator(nmix[...])
    shift_x = lax.rem(pos[0, 0], 3)
    shift_y = lax.rem(pos[0, 1], 3)
    span = (nest_cols, groups * LANES)
    table = hat(
        shift_y + lax.broadcasted_iota(jnp.int32, span, 0)
        - 3 * lax.broadcasted_iota(jnp.int32, span, 1)
    )
    first = t == 0

    @pl.when(t > 0)
    def _():
        halo_copy().wait_recv()

    for q in range(nt):
        @pl.when(t == q)
        def _():
            for r in range(nt):
                if r != q and needs(r, q):
                    spread_copy(r, q).wait_recv()

    lines = [
        jnp.dot(
            table, rows[i],
            precision=HIGH, preferred_element_type=jnp.float32,
        )
        for i in range(count)
    ]
    base = t * nest_rows
    lowest = jnp.clip(low_row(t), 0, win - count)
    total = nest_rows + STEPS
    for k in range(total):
        interp = None
        for i in range(count):
            weight = hat(shift_x + base - STEPS + k - 3 * (lowest + i))
            term = weight * lines[i]
            interp = term if interp is None else interp + term
        own = halo[k] if k < STEPS else state[k - STEPS]
        value = 0.5 * (own + interp)
        if k == STEPS:
            top = value
        current[k, PAD:] = value
        current[k, PAD - 1:PAD] = value[0:1]

    current[STEPS - 1, PAD:] = jnp.where(first, top, current[STEPS - 1, PAD:])
    along_x = courant[0:1]
    along_y = courant[1:2]
    for step in range(STEPS):
        value = current[step + 1:, PAD:]
        upper = current[step:total - 1, PAD:]
        left = current[step + 1:, PAD - 1:PAD - 1 + nest_cols]
        mixed = apply_operator(value.reshape(-1, width), operator).reshape(value.shape)
        value = value + along_x * (upper - value) + along_y * (left - value) + mixed
        current[step + 1:, PAD:] = value
        if step < STEPS - 1:
            current[STEPS - 1, PAD:] = jnp.where(first, top, value[STEPS - 2 - step])

    lead_x = lax.rem(3 - lax.rem(shift_x + base, 3), 3)
    lead_y = lax.rem(3 - shift_y, 3)
    cells = feed.shape[2]
    pick = (
        lax.broadcasted_iota(jnp.int32, (cells, nest_cols), 1)
        == lead_y + 3 * lax.broadcasted_iota(jnp.int32, (cells, nest_cols), 0)
    ).astype(jnp.float32)
    r0, r1, r2, r3 = (current[STEPS + i, PAD:] for i in range(nest_rows))
    chosen = jnp.where(lead_x == 0, r0, jnp.where(lead_x == 1, r1, r2))
    feed[t, 0] = jnp.dot(pick, chosen, precision=HIGH, preferred_element_type=jnp.float32)
    feed[t, 1] = jnp.dot(pick, r3, precision=HIGH, preferred_element_type=jnp.float32)

    hi, lo = t // lo_count, lax.rem(t, lo_count)

    def feed_copy(source, target, slot):
        return remote(feed.at[source], feed.at[source], send4.at[slot], recv4.at[source], target, n)

    sends = []
    for step in range(1, hi_count):
        sends.append(feed_copy(t, lax.rem(hi + step, hi_count) * lo_count + lo, len(sends)))
        sends[-1].start()
    for step in range(1, lo_count):
        sends.append(feed_copy(t, hi * lo_count + lax.rem(lo + step, lo_count), len(sends)))
        sends[-1].start()

    nest_out[...] = current[STEPS:, PAD:]
    lax.fori_loop(marks[3], marks[4], parent_rows, 0)

    for step in range(1, hi_count):
        source = lax.rem(hi + step, hi_count) * lo_count + lo
        feed_copy(source, t, 0).wait_recv()
        for across in range(1, lo_count):
            target = hi * lo_count + lax.rem(lo + across, lo_count)
            sends.append(feed_copy(source, target, len(sends)))
            sends[-1].start()

    lax.fori_loop(marks[4], marks[5], parent_rows, 0)

    @pl.when(t > 0)
    def _():
        down_copy().wait_recv()

    @pl.when(t < nt - 1)
    def _():
        up_copy().wait_recv()

    @pl.when(n > 0)
    def _():
        right_copy().wait_recv()

    @pl.when(n < nn - 1)
    def _():
        left_copy().wait_recv()

    fresh[0] += KAPPA * above[...]
    fresh[tile_rows - 1] += KAPPA * below[...]
    fresh[:, 0] += KAPPA * beside[0]
    fresh[:, tile_cols - 1] += KAPPA * beside[1]

    for across in range(1, lo_count):
        for step in range(hi_count):
            source = lax.rem(hi + step, hi_count) * lo_count + lax.rem(lo + across, lo_count)
            feed_copy(source, t, 0).wait_recv()

    for copy in sends:
        copy.wait_send()
    for r in range(nt):
        @pl.when(t == r)
        def _():
            for q in range(nt):
                if q != r and needs(r, q):
                    spread_copy(r, q).wait_send()
            for other in same_lo(r):
                gather_copy(r, other).wait_send()
            for other in same_hi(r):
                for chunk in range(hi_count):
                    early_copy(r, other, chunk).wait_send()

    @pl.when(t < nt - 1)
    def _():
        halo_copy().wait_send()
        down_copy().wait_send()

    @pl.when(t > 0)
    def _():
        up_copy().wait_send()

    @pl.when(n < nn - 1)
    def _():
        right_copy().wait_send()

    @pl.when(n > 0)
    def _():
        left_copy().wait_send()


def feedback_kernel(
    nest_rows, nest_total, nest_cols, pos, fresh, feed, nest, out, nest_out, patch, store, patched
):
    tile_rows, cols, width = fresh.shape
    share = tile_rows // LOADS
    copies = [
        pltpu.make_async_copy(
            fresh.at[pl.ds(i * share, share)], out.at[pl.ds(i * share, share)], store.at[i]
        )
        for i in range(LOADS)
    ]
    copies.append(pltpu.make_async_copy(nest, nest_out.at[0], store.at[LOADS]))
    for copy in copies:
        copy.start()
    lead_x = lax.rem(3 - lax.rem(pos[0, 0], 3), 3)
    lead_y = lax.rem(3 - lax.rem(pos[0, 1], 3), 3)
    top = (pos[0, 0] + lead_x) // 3 - lax.axis_index("tiles") * tile_rows
    first_col = (pos[0, 1] + lead_y) // 3 - lax.axis_index("nests") * cols
    window = patch.shape[1]
    base_col = pl.multiple_of(jnp.clip(first_col // 8 * 8, 0, cols - window), 8)
    offset = first_col - base_col
    limit = (nest_cols - lead_y + 2) // 3
    cell = lax.broadcasted_iota(jnp.int32, (window, width), 0) - offset
    live = (cell >= 0) & (cell < limit)

    def fed(k):
        return (lead_x + 3 * k < nest_total) & (top + k >= 0) & (top + k < tile_rows)

    def patch_copy(k):
        return pltpu.make_async_copy(
            patch.at[k], out.at[top + k, pl.ds(base_col, window)], patched.at[k]
        )

    for k in range(patch.shape[0]):
        @pl.when(fed(k))
        def _():
            x = lead_x + 3 * k
            sender = x // nest_rows
            slot = (x - sender * nest_rows) // 3
            values = jnp.concatenate(
                [feed[sender, slot], jnp.zeros((8, width), jnp.float32)], axis=0
            )
            values = pltpu.roll(values, offset, 0)
            old = fresh[top + k, pl.ds(base_col, window)]
            patch[k] = jnp.where(live, old + 0.5 * (values - old), old)

    for copy in copies:
        copy.wait()
    for k in range(patch.shape[0]):
        @pl.when(fed(k))
        def _():
            patch_copy(k).start()
    for k in range(patch.shape[0]):
        @pl.when(fed(k))
        def _():
            patch_copy(k).wait()


def shards(nt, nn, parent, nest_state, parent_mix, nest_mix, courant, nest_pos):
    tile_rows, tile_cols, width = parent.shape
    _, nest_rows, nest_cols, _ = nest_state.shape
    nest_total = nest_rows * nt
    win = (nest_total + 1) // 3 + 2
    need = (nest_cols + 1) // 3 + 2
    span = -(-need // LANES) * LANES
    groups = span // LANES
    count = -(-(nest_rows + STEPS + 1) // 3) + 2
    fb_cols = -(-((nest_cols + 2) // 3) // LANES) * LANES
    lo_count = nt // 4
    slots = (nest_rows + 2) // 3
    hi_count = nt // lo_count
    part_rows = -(-win // hi_count)
    part_cols = -(-groups // lo_count) * LANES
    vmem = pl.BlockSpec(memory_space=pltpu.VMEM)
    smem = pl.BlockSpec(memory_space=pltpu.SMEM)
    hbm = pl.BlockSpec(memory_space=pltpu.HBM)
    f32 = jnp.float32
    dma = pltpu.SemaphoreType.DMA
    nest_pos, parent, nest_state, parent_mix, nest_mix, courant = (
        pltpu.with_memory_space_constraint(array, pltpu.HBM)
        for array in (nest_pos, parent, nest_state, parent_mix, nest_mix, courant)
    )
    nest_new, feed, parent_new = pl.pallas_call(
        functools.partial(exchange_kernel, nt, nn, lo_count),
        out_shape=(
            jax.ShapeDtypeStruct((nest_rows, nest_cols, width), f32),
            jax.ShapeDtypeStruct((nt, slots, fb_cols, width), f32),
            pltpu.VMEM(parent.shape, f32),
        ),
        in_specs=[smem] + [hbm] * 5,
        out_specs=(vmem, vmem, vmem),
        scratch_shapes=[
            pltpu.VMEM((tile_rows + 2, tile_cols + 2 * PAD, width), f32),
            pltpu.VMEM((win, span, width), f32),
            pltpu.VMEM((2, tile_rows, width), f32),
            pltpu.VMEM((tile_cols, width), f32),
            pltpu.VMEM((tile_cols, width), f32),
            pltpu.VMEM((2, tile_rows, width), f32),
            pltpu.VMEM((nest_rows, nest_cols, width), f32),
            pltpu.VMEM((width, width), f32),
            pltpu.VMEM((width, width), f32),
            pltpu.VMEM((2, width), f32),
            pltpu.VMEM((lo_count, win, part_cols, width), f32),
            pltpu.VMEM((win, part_cols, width), f32),
            pltpu.VMEM((hi_count, part_rows, part_cols, width), f32),
            pltpu.VMEM((part_rows, part_cols, width), f32),
            pltpu.VMEM((count, span, width), f32),
            pltpu.VMEM((STEPS, nest_cols, width), f32),
            pltpu.VMEM((nest_rows + STEPS, nest_cols + PAD, width), f32),
            dma((LOADS + 4,)),
            dma((lo_count, hi_count)), dma((lo_count, hi_count)),
            dma((hi_count,)), dma((hi_count,)), dma((nt,)), dma((nt,)),
            dma((5,)), dma((5,)), dma((nt - 1,)), dma((nt,)),
        ],
        compiler_params=pltpu.CompilerParams(
            collective_id=0, has_side_effects=True, vmem_limit_bytes=VMEM_LIMIT
        ),
        name="nest_exchange",
    )(nest_pos, parent, nest_state, parent_mix, nest_mix, courant)

    fed_rows = (nest_total + 2) // 3
    parent_new = pltpu.with_memory_space_constraint(parent_new, pltpu.VMEM)
    return pl.pallas_call(
        functools.partial(feedback_kernel, nest_rows, nest_total, nest_cols),
        out_shape=(
            jax.ShapeDtypeStruct(parent.shape, f32),
            jax.ShapeDtypeStruct(nest_state.shape, f32),
        ),
        in_specs=[smem, vmem, vmem, vmem],
        out_specs=(hbm, hbm),
        scratch_shapes=[
            pltpu.VMEM((fed_rows, fb_cols + 8, width), f32),
            dma((LOADS + 1,)), dma((fed_rows,)),
        ],
        compiler_params=pltpu.CompilerParams(vmem_limit_bytes=FEED_LIMIT),
        name="feedback",
    )(nest_pos, parent_new, feed, nest_new)


def solution(mesh):
    placed = (
        P("tiles", "nests", None),
        P("nests", "tiles", None, None),
        P(),
        P(),
        P(),
        P("nests", None),
    )
    return jax.shard_map(
        functools.partial(shards, mesh.shape["tiles"], mesh.shape["nests"]),
        mesh=mesh,
        in_specs=placed,
        out_specs=(P("tiles", "nests", None), P("nests", "tiles", None, None)),
        check_vma=False,
    )
```

```python
import functools

import jax
import jax.numpy as jnp
from jax import lax
from jax.experimental import pallas as pl
from jax.experimental.pallas import tpu as pltpu
from jax.sharding import PartitionSpec as P

STEPS = 3
KAPPA = 0.125
MESH = pl.DeviceIdType.MESH
LANES = 8
CHUNK = 4
GROUP = 2
LOADS = 4
PAD = 8
VMEM_LIMIT = 40 * 1024 * 1024
FEED_LIMIT = 16 * 1024 * 1024


def split_operator(mix):
    high = mix.astype(jnp.bfloat16)
    low = (mix - high.astype(jnp.float32)).astype(jnp.bfloat16)
    upper = jnp.concatenate([high, low], axis=1)
    lower = jnp.concatenate([high, jnp.zeros_like(low)], axis=1)
    return jnp.concatenate([upper, lower], axis=0)


def apply_operator(values, operator):
    width = values.shape[-1]
    high = values.astype(jnp.bfloat16)
    low = (values - high.astype(jnp.float32)).astype(jnp.bfloat16)
    both = jnp.dot(
        jnp.concatenate([high, low], axis=1), operator, preferred_element_type=jnp.float32
    )
    return both[:, :width] + both[:, width:]


def hat(distance):
    return jnp.maximum(3 - jnp.abs(distance), 0).astype(jnp.float32)


def apply_table(table, values):
    width = values.shape[-1]
    high = values.astype(jnp.bfloat16)
    low = (values - high.astype(jnp.float32)).astype(jnp.bfloat16)
    both = jnp.dot(
        table.astype(jnp.bfloat16), jnp.concatenate([high, low], axis=1),
        preferred_element_type=jnp.float32,
    )
    return both[:, :width] + both[:, width:]


def exchange_kernel(
    nt, nn, lo_count, pos, parent_hbm, state_hbm, pmix_hbm, nmix_hbm, courant_hbm,
    nest_out, feed, fresh,
    held, band, edges, above, below, beside, state, pmix, nmix, courant,
    arrived, reduced, rows, halo, current,
    load, send1, recv1, send2, recv2, send3, recv3, send4, recv4,
):
    t = lax.axis_index("tiles")
    n = lax.axis_index("nests")
    nest_rows, nest_cols, width = state.shape
    tile_rows, tile_cols, _ = fresh.shape
    win, span, _ = band.shape
    groups = span // LANES
    count = rows.shape[0]

    def low_row(tile):
        return (tile * nest_rows - STEPS + 3) // 3 - 1

    def cut(extent, parts, index):
        return extent * index // parts, extent * (index + 1) // parts

    lows = [min(max(low_row(tile), 0), win - count) for tile in range(nt)]
    parts = []
    for tile in range(nt):
        row_a, row_b = (-(-win * i // (nt // lo_count)) for i in (tile // lo_count, tile // lo_count + 1))
        col_a, col_b = cut(groups, lo_count, tile % lo_count)
        parts.append((row_a, row_b, col_a * LANES, col_b * LANES))

    def overlap(source, target):
        low = max(parts[source][0], lows[target])
        high = min(parts[source][1], lows[target] + count)
        return low, high

    def remote(src, dst, send, recv, tile, nest):
        return pltpu.make_async_remote_copy(
            src_ref=src, dst_ref=dst, send_sem=send, recv_sem=recv,
            device_id=(tile, nest), device_id_type=MESH,
        )

    share = tile_rows // LOADS
    parent_loads = [
        pltpu.make_async_copy(
            parent_hbm.at[pl.ds(i * share, share)],
            held.at[pl.ds(1 + i * share, share), pl.ds(PAD, tile_cols)], load.at[i],
        )
        for i in range(LOADS)
    ]
    small_loads = [
        pltpu.make_async_copy(pmix_hbm, pmix, load.at[LOADS]),
        pltpu.make_async_copy(state_hbm.at[0], state, load.at[LOADS + 1]),
        pltpu.make_async_copy(nmix_hbm, nmix, load.at[LOADS + 2]),
        pltpu.make_async_copy(courant_hbm, courant, load.at[LOADS + 3]),
    ]
    for copy in parent_loads + small_loads:
        copy.start()

    barrier = pltpu.get_barrier_semaphore()
    for step in range(1, nt):
        pl.semaphore_signal(
            barrier, inc=1, device_id=(lax.rem(t + step, nt), n), device_id_type=MESH
        )

    @pl.when(n > 0)
    def _():
        pl.semaphore_signal(barrier, inc=1, device_id=(t, n - 1), device_id_type=MESH)

    @pl.when(n < nn - 1)
    def _():
        pl.semaphore_signal(barrier, inc=1, device_id=(t, n + 1), device_id_type=MESH)

    held[0] = jnp.zeros(held.shape[1:], jnp.float32)
    held[tile_rows + 1] = jnp.zeros(held.shape[1:], jnp.float32)
    strip = jnp.zeros((tile_rows, PAD, width), jnp.float32)
    held[1:tile_rows + 1, :PAD] = strip
    held[1:tile_rows + 1, PAD + tile_cols:] = strip

    @pl.when(t == 0)
    def _():
        halo[...] = jnp.zeros_like(halo)
        above[...] = jnp.zeros_like(above)

    @pl.when(t == nt - 1)
    def _():
        below[...] = jnp.zeros_like(below)

    @pl.when(n == 0)
    def _():
        beside[0] = jnp.zeros(beside.shape[1:], jnp.float32)

    @pl.when(n == nn - 1)
    def _():
        beside[1] = jnp.zeros(beside.shape[1:], jnp.float32)

    peers = nt - 1 + (n > 0).astype(jnp.int32) + (n < nn - 1).astype(jnp.int32)
    pl.semaphore_wait(barrier, peers)

    def halo_copy():
        return remote(
            state_hbm.at[0, pl.ds(nest_rows - STEPS, STEPS)], halo, send3.at[0], recv3.at[0],
            t + 1, n,
        )

    def down_copy():
        return remote(
            parent_hbm.at[tile_rows - 1], above, send3.at[1], recv3.at[1], t + 1, n
        )

    def up_copy():
        return remote(parent_hbm.at[0], below, send3.at[2], recv3.at[2], t - 1, n)

    def right_copy():
        return remote(edges.at[1], beside.at[0], send3.at[3], recv3.at[3], t, n + 1)

    def left_copy():
        return remote(edges.at[0], beside.at[1], send3.at[4], recv3.at[4], t, n - 1)

    @pl.when(t < nt - 1)
    def _():
        halo_copy().start()

    @pl.when(t > 0)
    def _():
        up_copy().start()

    for copy in parent_loads:
        copy.wait()

    local = pos[0, 0] // 3 - t * tile_rows
    corner = jnp.clip(pos[0, 1] // 3 - n * tile_cols, 0, tile_cols - span)
    for w in range(win):
        row = local + w
        inside = (row >= 0) & (row < tile_rows)
        part = held[jnp.clip(row, 0, tile_rows - 1) + 1, pl.ds(PAD + corner, span)]
        band[w] = jnp.where(inside, part, 0.0)

    def gather_copy(source, target):
        row_a, row_b, col_a, col_b = parts[target]
        return remote(
            band.at[row_a:row_b, col_a:col_b],
            arrived.at[source, 0:row_b - row_a, 0:col_b - col_a],
            send1.at[target], recv1.at[source], target, n,
        )

    for r in range(nt):
        @pl.when(t != r)
        def _():
            gather_copy(t, r).start()

    edges[0] = held[1:tile_rows + 1, PAD]
    edges[1] = held[1:tile_rows + 1, PAD + tile_cols - 1]

    @pl.when(n < nn - 1)
    def _():
        right_copy().start()

    @pl.when(n > 0)
    def _():
        left_copy().start()

    for copy in small_loads:
        copy.wait()
    parent_operator = split_operator(pmix[...])

    def parent_rows(step, carry):
        for i in range(0, CHUNK, GROUP):
            row = step * CHUNK + i
            value = held[pl.ds(row + 1, GROUP), PAD:PAD + tile_cols]
            around = (
                held[pl.ds(row, GROUP), PAD:PAD + tile_cols]
                + held[pl.ds(row + 2, GROUP), PAD:PAD + tile_cols]
                + held[pl.ds(row + 1, GROUP), PAD + 1:PAD + 1 + tile_cols]
                + held[pl.ds(row + 1, GROUP), PAD - 1:PAD - 1 + tile_cols]
            )
            mixed = apply_operator(value.reshape(GROUP * tile_cols, width), parent_operator)
            fresh[pl.ds(row, GROUP)] = (
                value + KAPPA * (around - 4.0 * value) + mixed.reshape(value.shape)
            )
        return carry

    chunks = tile_rows // CHUNK
    marks = [0, chunks * 9 // 16, chunks * 12 // 16, chunks * 14 // 16, chunks]
    lax.fori_loop(marks[0], marks[1], parent_rows, 0)

    def spread_copy(source, target):
        row_a, _, col_a, col_b = parts[source]
        low, high = overlap(source, target)
        return remote(
            reduced.at[low - row_a:high - row_a, 0:col_b - col_a],
            rows.at[low - lows[target]:high - lows[target], col_a:col_b],
            send2.at[target], recv2.at[source], target, n,
        )

    def needs(source, target):
        low, high = overlap(source, target)
        return low < high and parts[source][2] < parts[source][3]

    for r in range(nt):
        row_a, row_b, col_a, col_b = parts[r]

        @pl.when(t == r)
        def _():
            total = band[row_a:row_b, col_a:col_b]
            for s in range(nt):
                if s != r:
                    gather_copy(s, r).wait_recv()
                    total = total + arrived[s, 0:row_b - row_a, 0:col_b - col_a]
            reduced[0:row_b - row_a, 0:col_b - col_a] = total
            for q in range(nt):
                if q != r and needs(r, q):
                    spread_copy(r, q).start()
            low, high = overlap(r, r)
            if needs(r, r):
                rows[low - lows[r]:high - lows[r], col_a:col_b] = (
                    reduced[low - row_a:high - row_a, 0:col_b - col_a]
                )

    lax.fori_loop(marks[1], marks[2], parent_rows, 0)

    operator = split_operator(nmix[...])
    shift_x = lax.rem(pos[0, 0], 3)
    shift_y = lax.rem(pos[0, 1], 3)
    span = (nest_cols, groups * LANES)
    table = hat(
        shift_y + lax.broadcasted_iota(jnp.int32, span, 0)
        - 3 * lax.broadcasted_iota(jnp.int32, span, 1)
    )
    first = t == 0

    @pl.when(t > 0)
    def _():
        halo_copy().wait_recv()

    for q in range(nt):
        @pl.when(t == q)
        def _():
            for r in range(nt):
                if r != q and needs(r, q):
                    spread_copy(r, q).wait_recv()

    lines = [apply_table(table, rows[i]) * (1.0 / 9.0) for i in range(count)]
    base = t * nest_rows
    lowest = jnp.clip(low_row(t), 0, win - count)
    total = nest_rows + STEPS
    for k in range(total):
        interp = None
        for i in range(count):
            weight = hat(shift_x + base - STEPS + k - 3 * (lowest + i))
            term = weight * lines[i]
            interp = term if interp is None else interp + term
        own = halo[k] if k < STEPS else state[k - STEPS]
        value = 0.5 * (own + interp)
        if k == STEPS:
            top = value
        current[k, PAD:] = value
        current[k, PAD - 1:PAD] = value[0:1]

    current[STEPS - 1, PAD:] = jnp.where(first, top, current[STEPS - 1, PAD:])
    along_x = courant[0:1]
    along_y = courant[1:2]
    for step in range(STEPS):
        value = current[step + 1:, PAD:]
        upper = current[step:total - 1, PAD:]
        left = current[step + 1:, PAD - 1:PAD - 1 + nest_cols]
        mixed = apply_operator(value.reshape(-1, width), operator).reshape(value.shape)
        value = value + along_x * (upper - value) + along_y * (left - value) + mixed
        current[step + 1:, PAD:] = value
        if step < STEPS - 1:
            current[STEPS - 1, PAD:] = jnp.where(first, top, value[STEPS - 2 - step])

    lead_x = lax.rem(3 - lax.rem(shift_x + base, 3), 3)
    lead_y = lax.rem(3 - shift_y, 3)
    cells = feed.shape[2]
    pick = (
        lax.broadcasted_iota(jnp.int32, (cells, nest_cols), 1)
        == lead_y + 3 * lax.broadcasted_iota(jnp.int32, (cells, nest_cols), 0)
    ).astype(jnp.float32)
    r0, r1, r2, r3 = (current[STEPS + i, PAD:] for i in range(nest_rows))
    chosen = jnp.where(lead_x == 0, r0, jnp.where(lead_x == 1, r1, r2))
    feed[t, 0] = apply_table(pick, chosen)
    feed[t, 1] = apply_table(pick, r3)

    hi_count = nt // lo_count
    hi, lo = t // lo_count, lax.rem(t, lo_count)

    def feed_copy(source, target, slot):
        return remote(feed.at[source], feed.at[source], send4.at[slot], recv4.at[source], target, n)

    sends = []
    for step in range(1, hi_count):
        sends.append(feed_copy(t, lax.rem(hi + step, hi_count) * lo_count + lo, len(sends)))
        sends[-1].start()
    for step in range(1, lo_count):
        sends.append(feed_copy(t, hi * lo_count + lax.rem(lo + step, lo_count), len(sends)))
        sends[-1].start()

    @pl.when(t < nt - 1)
    def _():
        down_copy().start()

    nest_out[...] = current[STEPS:, PAD:]
    lax.fori_loop(marks[2], marks[3], parent_rows, 0)

    for step in range(1, hi_count):
        source = lax.rem(hi + step, hi_count) * lo_count + lo
        feed_copy(source, t, 0).wait_recv()
        for across in range(1, lo_count):
            target = hi * lo_count + lax.rem(lo + across, lo_count)
            sends.append(feed_copy(source, target, len(sends)))
            sends[-1].start()

    lax.fori_loop(marks[3], marks[4], parent_rows, 0)

    @pl.when(t > 0)
    def _():
        down_copy().wait_recv()

    @pl.when(t < nt - 1)
    def _():
        up_copy().wait_recv()

    @pl.when(n > 0)
    def _():
        right_copy().wait_recv()

    @pl.when(n < nn - 1)
    def _():
        left_copy().wait_recv()

    fresh[0] += KAPPA * above[...]
    fresh[tile_rows - 1] += KAPPA * below[...]
    fresh[:, 0] += KAPPA * beside[0]
    fresh[:, tile_cols - 1] += KAPPA * beside[1]

    for across in range(1, lo_count):
        for step in range(hi_count):
            source = lax.rem(hi + step, hi_count) * lo_count + lax.rem(lo + across, lo_count)
            feed_copy(source, t, 0).wait_recv()

    for copy in sends:
        copy.wait_send()
    for r in range(nt):
        @pl.when(t != r)
        def _():
            gather_copy(t, r).wait_send()

        @pl.when(t == r)
        def _():
            for q in range(nt):
                if q != r and needs(r, q):
                    spread_copy(r, q).wait_send()

    @pl.when(t < nt - 1)
    def _():
        halo_copy().wait_send()
        down_copy().wait_send()

    @pl.when(t > 0)
    def _():
        up_copy().wait_send()

    @pl.when(n < nn - 1)
    def _():
        right_copy().wait_send()

    @pl.when(n > 0)
    def _():
        left_copy().wait_send()


def feedback_kernel(
    nest_rows, nest_total, nest_cols, pos, fresh, feed, nest, out, nest_out, patch, store, patched
):
    tile_rows, cols, width = fresh.shape
    share = tile_rows // LOADS
    copies = [
        pltpu.make_async_copy(
            fresh.at[pl.ds(i * share, share)], out.at[pl.ds(i * share, share)], store.at[i]
        )
        for i in range(LOADS)
    ]
    copies.append(pltpu.make_async_copy(nest, nest_out.at[0], store.at[LOADS]))
    for copy in copies:
        copy.start()
    lead_x = lax.rem(3 - lax.rem(pos[0, 0], 3), 3)
    lead_y = lax.rem(3 - lax.rem(pos[0, 1], 3), 3)
    top = (pos[0, 0] + lead_x) // 3 - lax.axis_index("tiles") * tile_rows
    first_col = (pos[0, 1] + lead_y) // 3 - lax.axis_index("nests") * cols
    window = patch.shape[1]
    base_col = pl.multiple_of(jnp.clip(first_col // 8 * 8, 0, cols - window), 8)
    offset = first_col - base_col
    limit = (nest_cols - lead_y + 2) // 3
    cell = lax.broadcasted_iota(jnp.int32, (window, width), 0) - offset
    live = (cell >= 0) & (cell < limit)

    def fed(k):
        return (lead_x + 3 * k < nest_total) & (top + k >= 0) & (top + k < tile_rows)

    def patch_copy(k):
        return pltpu.make_async_copy(
            patch.at[k], out.at[top + k, pl.ds(base_col, window)], patched.at[k]
        )

    for k in range(patch.shape[0]):
        @pl.when(fed(k))
        def _():
            x = lead_x + 3 * k
            sender = x // nest_rows
            slot = (x - sender * nest_rows) // 3
            values = jnp.concatenate(
                [feed[sender, slot], jnp.zeros((8, width), jnp.float32)], axis=0
            )
            values = pltpu.roll(values, offset, 0)
            old = fresh[top + k, pl.ds(base_col, window)]
            patch[k] = jnp.where(live, old + 0.5 * (values - old), old)

    for copy in copies:
        copy.wait()
    for k in range(patch.shape[0]):
        @pl.when(fed(k))
        def _():
            patch_copy(k).start()
    for k in range(patch.shape[0]):
        @pl.when(fed(k))
        def _():
            patch_copy(k).wait()


def shards(nt, nn, parent, nest_state, parent_mix, nest_mix, courant, nest_pos):
    tile_rows, tile_cols, width = parent.shape
    _, nest_rows, nest_cols, _ = nest_state.shape
    nest_total = nest_rows * nt
    win = (nest_total + 1) // 3 + 2
    need = (nest_cols + 1) // 3 + 2
    span = -(-need // LANES) * LANES
    groups = span // LANES
    count = -(-(nest_rows + STEPS + 1) // 3) + 2
    fb_cols = -(-((nest_cols + 2) // 3) // LANES) * LANES
    lo_count = nt // 4
    slots = (nest_rows + 2) // 3
    part_rows = -(-win // (nt // lo_count))
    part_cols = -(-groups // lo_count) * LANES
    vmem = pl.BlockSpec(memory_space=pltpu.VMEM)
    smem = pl.BlockSpec(memory_space=pltpu.SMEM)
    hbm = pl.BlockSpec(memory_space=pltpu.HBM)
    f32 = jnp.float32
    dma = pltpu.SemaphoreType.DMA
    nest_pos, parent, nest_state, parent_mix, nest_mix, courant = (
        pltpu.with_memory_space_constraint(array, pltpu.HBM)
        for array in (nest_pos, parent, nest_state, parent_mix, nest_mix, courant)
    )
    nest_new, feed, parent_new = pl.pallas_call(
        functools.partial(exchange_kernel, nt, nn, lo_count),
        out_shape=(
            jax.ShapeDtypeStruct((nest_rows, nest_cols, width), f32),
            jax.ShapeDtypeStruct((nt, slots, fb_cols, width), f32),
            pltpu.VMEM(parent.shape, f32),
        ),
        in_specs=[smem] + [hbm] * 5,
        out_specs=(vmem, vmem, vmem),
        scratch_shapes=[
            pltpu.VMEM((tile_rows + 2, tile_cols + 2 * PAD, width), f32),
            pltpu.VMEM((win, span, width), f32),
            pltpu.VMEM((2, tile_rows, width), f32),
            pltpu.VMEM((tile_cols, width), f32),
            pltpu.VMEM((tile_cols, width), f32),
            pltpu.VMEM((2, tile_rows, width), f32),
            pltpu.VMEM((nest_rows, nest_cols, width), f32),
            pltpu.VMEM((width, width), f32),
            pltpu.VMEM((width, width), f32),
            pltpu.VMEM((2, width), f32),
            pltpu.VMEM((nt, part_rows, part_cols, width), f32),
            pltpu.VMEM((part_rows, part_cols, width), f32),
            pltpu.VMEM((count, span, width), f32),
            pltpu.VMEM((STEPS, nest_cols, width), f32),
            pltpu.VMEM((nest_rows + STEPS, nest_cols + PAD, width), f32),
            dma((LOADS + 4,)),
            dma((nt,)), dma((nt,)), dma((nt,)), dma((nt,)),
            dma((5,)), dma((5,)), dma((nt - 1,)), dma((nt,)),
        ],
        compiler_params=pltpu.CompilerParams(
            collective_id=0, has_side_effects=True, vmem_limit_bytes=VMEM_LIMIT
        ),
        name="nest_exchange",
    )(nest_pos, parent, nest_state, parent_mix, nest_mix, courant)

    fed_rows = (nest_total + 2) // 3
    parent_new = pltpu.with_memory_space_constraint(parent_new, pltpu.VMEM)
    return pl.pallas_call(
        functools.partial(feedback_kernel, nest_rows, nest_total, nest_cols),
        out_shape=(
            jax.ShapeDtypeStruct(parent.shape, f32),
            jax.ShapeDtypeStruct(nest_state.shape, f32),
        ),
        in_specs=[smem, vmem, vmem, vmem],
        out_specs=(hbm, hbm),
        scratch_shapes=[
            pltpu.VMEM((fed_rows, fb_cols + 8, width), f32),
            dma((LOADS + 1,)), dma((fed_rows,)),
        ],
        compiler_params=pltpu.CompilerParams(vmem_limit_bytes=FEED_LIMIT),
        name="feedback",
    )(nest_pos, parent_new, feed, nest_new)


def solution(mesh):
    placed = (
        P("tiles", "nests", None),
        P("nests", "tiles", None, None),
        P(),
        P(),
        P(),
        P("nests", None),
    )
    return jax.shard_map(
        functools.partial(shards, mesh.shape["tiles"], mesh.shape["nests"]),
        mesh=mesh,
        in_specs=placed,
        out_specs=(P("tiles", "nests", None), P("nests", "tiles", None, None)),
        check_vma=False,
    )
```

```python
import functools

import jax
import jax.numpy as jnp
from jax import lax
from jax.experimental import pallas as pl
from jax.experimental.pallas import tpu as pltpu
from jax.sharding import PartitionSpec as P

STEPS = 3
KAPPA = 0.125
MESH = pl.DeviceIdType.MESH
LANES = 8
CHUNK = 4
GROUP = 2
LOADS = 4
PAD = 8
VMEM_LIMIT = 40 * 1024 * 1024
FEED_LIMIT = 16 * 1024 * 1024


def split_operator(mix):
    high = mix.astype(jnp.bfloat16)
    low = (mix - high.astype(jnp.float32)).astype(jnp.bfloat16)
    upper = jnp.concatenate([high, low], axis=1)
    lower = jnp.concatenate([high, jnp.zeros_like(low)], axis=1)
    return jnp.concatenate([upper, lower], axis=0)


def apply_operator(values, operator):
    width = values.shape[-1]
    high = values.astype(jnp.bfloat16)
    low = (values - high.astype(jnp.float32)).astype(jnp.bfloat16)
    both = jnp.dot(
        jnp.concatenate([high, low], axis=1), operator, preferred_element_type=jnp.float32
    )
    return both[:, :width] + both[:, width:]


def hat(distance):
    return jnp.maximum(3 - jnp.abs(distance), 0).astype(jnp.float32)


def apply_table(table, values):
    width = values.shape[-1]
    high = values.astype(jnp.bfloat16)
    low = (values - high.astype(jnp.float32)).astype(jnp.bfloat16)
    both = jnp.dot(
        table.astype(jnp.bfloat16), jnp.concatenate([high, low], axis=1),
        preferred_element_type=jnp.float32,
    )
    return both[:, :width] + both[:, width:]


def exchange_kernel(
    nt, nn, lo_count, pos, parent_hbm, state_hbm, pmix_hbm, nmix_hbm, courant_hbm,
    nest_out, feed, fresh,
    held, band, edges, above, below, beside, state, pmix, nmix, courant,
    arrived, reduced, rows, halo, current,
    load, send1, recv1, send2, recv2, send3, recv3, send4, recv4,
):
    t = lax.axis_index("tiles")
    n = lax.axis_index("nests")
    nest_rows, nest_cols, width = state.shape
    tile_rows, tile_cols, _ = fresh.shape
    win, span, _ = band.shape
    groups = span // LANES
    count = rows.shape[0]

    def low_row(tile):
        return (tile * nest_rows - STEPS + 3) // 3 - 1

    def cut(extent, parts, index):
        return extent * index // parts, extent * (index + 1) // parts

    lows = [min(max(low_row(tile), 0), win - count) for tile in range(nt)]
    parts = []
    for tile in range(nt):
        row_a, row_b = (-(-win * i // (nt // lo_count)) for i in (tile // lo_count, tile // lo_count + 1))
        col_a, col_b = cut(groups, lo_count, tile % lo_count)
        parts.append((row_a, row_b, col_a * LANES, col_b * LANES))

    def overlap(source, target):
        low = max(parts[source][0], lows[target])
        high = min(parts[source][1], lows[target] + count)
        return low, high

    def remote(src, dst, send, recv, tile, nest):
        return pltpu.make_async_remote_copy(
            src_ref=src, dst_ref=dst, send_sem=send, recv_sem=recv,
            device_id=(tile, nest), device_id_type=MESH,
        )

    share = tile_rows // LOADS
    parent_loads = [
        pltpu.make_async_copy(
            parent_hbm.at[pl.ds(i * share, share)],
            held.at[pl.ds(1 + i * share, share), pl.ds(PAD, tile_cols)], load.at[i],
        )
        for i in range(LOADS)
    ]
    small_loads = [
        pltpu.make_async_copy(pmix_hbm, pmix, load.at[LOADS]),
        pltpu.make_async_copy(state_hbm.at[0], state, load.at[LOADS + 1]),
        pltpu.make_async_copy(nmix_hbm, nmix, load.at[LOADS + 2]),
        pltpu.make_async_copy(courant_hbm, courant, load.at[LOADS + 3]),
    ]
    for copy in parent_loads + small_loads:
        copy.start()

    barrier = pltpu.get_barrier_semaphore()
    for step in range(1, nt):
        pl.semaphore_signal(
            barrier, inc=1, device_id=(lax.rem(t + step, nt), n), device_id_type=MESH
        )

    @pl.when(n > 0)
    def _():
        pl.semaphore_signal(barrier, inc=1, device_id=(t, n - 1), device_id_type=MESH)

    @pl.when(n < nn - 1)
    def _():
        pl.semaphore_signal(barrier, inc=1, device_id=(t, n + 1), device_id_type=MESH)

    held[0] = jnp.zeros(held.shape[1:], jnp.float32)
    held[tile_rows + 1] = jnp.zeros(held.shape[1:], jnp.float32)
    strip = jnp.zeros((tile_rows, PAD, width), jnp.float32)
    held[1:tile_rows + 1, :PAD] = strip
    held[1:tile_rows + 1, PAD + tile_cols:] = strip

    @pl.when(t == 0)
    def _():
        halo[...] = jnp.zeros_like(halo)
        above[...] = jnp.zeros_like(above)

    @pl.when(t == nt - 1)
    def _():
        below[...] = jnp.zeros_like(below)

    @pl.when(n == 0)
    def _():
        beside[0] = jnp.zeros(beside.shape[1:], jnp.float32)

    @pl.when(n == nn - 1)
    def _():
        beside[1] = jnp.zeros(beside.shape[1:], jnp.float32)

    peers = nt - 1 + (n > 0).astype(jnp.int32) + (n < nn - 1).astype(jnp.int32)
    pl.semaphore_wait(barrier, peers)

    def halo_copy():
        return remote(
            state_hbm.at[0, pl.ds(nest_rows - STEPS, STEPS)], halo, send3.at[0], recv3.at[0],
            t + 1, n,
        )

    def down_copy():
        return remote(
            parent_hbm.at[tile_rows - 1], above, send3.at[1], recv3.at[1], t + 1, n
        )

    def up_copy():
        return remote(parent_hbm.at[0], below, send3.at[2], recv3.at[2], t - 1, n)

    def right_copy():
        return remote(edges.at[1], beside.at[0], send3.at[3], recv3.at[3], t, n + 1)

    def left_copy():
        return remote(edges.at[0], beside.at[1], send3.at[4], recv3.at[4], t, n - 1)

    @pl.when(t < nt - 1)
    def _():
        halo_copy().start()

    @pl.when(t > 0)
    def _():
        up_copy().start()

    for copy in parent_loads:
        copy.wait()

    local = pos[0, 0] // 3 - t * tile_rows
    corner = jnp.clip(pos[0, 1] // 3 - n * tile_cols, 0, tile_cols - span)
    for w in range(win):
        row = local + w
        inside = (row >= 0) & (row < tile_rows)
        part = held[jnp.clip(row, 0, tile_rows - 1) + 1, pl.ds(PAD + corner, span)]
        band[w] = jnp.where(inside, part, 0.0)

    def gather_copy(source, target):
        row_a, row_b, col_a, col_b = parts[target]
        return remote(
            band.at[row_a:row_b, col_a:col_b],
            arrived.at[source, 0:row_b - row_a, 0:col_b - col_a],
            send1.at[target], recv1.at[source], target, n,
        )

    for r in range(nt):
        @pl.when(t != r)
        def _():
            gather_copy(t, r).start()

    edges[0] = held[1:tile_rows + 1, PAD]
    edges[1] = held[1:tile_rows + 1, PAD + tile_cols - 1]

    @pl.when(n < nn - 1)
    def _():
        right_copy().start()

    @pl.when(n > 0)
    def _():
        left_copy().start()

    for copy in small_loads:
        copy.wait()
    parent_operator = split_operator(pmix[...])

    def parent_rows(step, carry):
        for i in range(0, CHUNK, GROUP):
            row = step * CHUNK + i
            value = held[pl.ds(row + 1, GROUP), PAD:PAD + tile_cols]
            around = (
                held[pl.ds(row, GROUP), PAD:PAD + tile_cols]
                + held[pl.ds(row + 2, GROUP), PAD:PAD + tile_cols]
                + held[pl.ds(row + 1, GROUP), PAD + 1:PAD + 1 + tile_cols]
                + held[pl.ds(row + 1, GROUP), PAD - 1:PAD - 1 + tile_cols]
            )
            mixed = apply_operator(value.reshape(GROUP * tile_cols, width), parent_operator)
            fresh[pl.ds(row, GROUP)] = (
                value + KAPPA * (around - 4.0 * value) + mixed.reshape(value.shape)
            )
        return carry

    chunks = tile_rows // CHUNK
    marks = [0, chunks * 9 // 16, chunks * 12 // 16, chunks * 14 // 16, chunks]
    lax.fori_loop(marks[0], marks[1], parent_rows, 0)

    def spread_copy(source, target):
        row_a, _, col_a, col_b = parts[source]
        low, high = overlap(source, target)
        return remote(
            reduced.at[low - row_a:high - row_a, 0:col_b - col_a],
            rows.at[low - lows[target]:high - lows[target], col_a:col_b],
            send2.at[target], recv2.at[source], target, n,
        )

    def needs(source, target):
        low, high = overlap(source, target)
        return low < high and parts[source][2] < parts[source][3]

    for r in range(nt):
        row_a, row_b, col_a, col_b = parts[r]

        @pl.when(t == r)
        def _():
            total = band[row_a:row_b, col_a:col_b]
            for s in range(nt):
                if s != r:
                    gather_copy(s, r).wait_recv()
                    total = total + arrived[s, 0:row_b - row_a, 0:col_b - col_a]
            reduced[0:row_b - row_a, 0:col_b - col_a] = total
            for q in range(nt):
                if q != r and needs(r, q):
                    spread_copy(r, q).start()
            low, high = overlap(r, r)
            if needs(r, r):
                rows[low - lows[r]:high - lows[r], col_a:col_b] = (
                    reduced[low - row_a:high - row_a, 0:col_b - col_a]
                )

    @pl.when(t < nt - 1)
    def _():
        down_copy().start()

    lax.fori_loop(marks[1], marks[2], parent_rows, 0)

    operator = split_operator(nmix[...])
    shift_x = lax.rem(pos[0, 0], 3)
    shift_y = lax.rem(pos[0, 1], 3)
    span = (nest_cols, groups * LANES)
    table = hat(
        shift_y + lax.broadcasted_iota(jnp.int32, span, 0)
        - 3 * lax.broadcasted_iota(jnp.int32, span, 1)
    )
    first = t == 0

    @pl.when(t > 0)
    def _():
        halo_copy().wait_recv()

    for q in range(nt):
        @pl.when(t == q)
        def _():
            for r in range(nt):
                if r != q and needs(r, q):
                    spread_copy(r, q).wait_recv()

    lines = [apply_table(table, rows[i]) * (1.0 / 9.0) for i in range(count)]
    base = t * nest_rows
    lowest = jnp.clip(low_row(t), 0, win - count)
    total = nest_rows + STEPS
    for k in range(total):
        interp = None
        for i in range(count):
            weight = hat(shift_x + base - STEPS + k - 3 * (lowest + i))
            term = weight * lines[i]
            interp = term if interp is None else interp + term
        own = halo[k] if k < STEPS else state[k - STEPS]
        value = 0.5 * (own + interp)
        if k == STEPS:
            top = value
        current[k, PAD:] = value
        current[k, PAD - 1:PAD] = value[0:1]

    current[STEPS - 1, PAD:] = jnp.where(first, top, current[STEPS - 1, PAD:])
    along_x = courant[0:1]
    along_y = courant[1:2]
    for step in range(STEPS):
        value = current[step + 1:, PAD:]
        upper = current[step:total - 1, PAD:]
        left = current[step + 1:, PAD - 1:PAD - 1 + nest_cols]
        mixed = apply_operator(value.reshape(-1, width), operator).reshape(value.shape)
        value = value + along_x * (upper - value) + along_y * (left - value) + mixed
        current[step + 1:, PAD:] = value
        if step < STEPS - 1:
            current[STEPS - 1, PAD:] = jnp.where(first, top, value[STEPS - 2 - step])

    lead_x = lax.rem(3 - lax.rem(shift_x + base, 3), 3)
    lead_y = lax.rem(3 - shift_y, 3)
    cells = feed.shape[2]
    pick = (
        lax.broadcasted_iota(jnp.int32, (cells, nest_cols), 1)
        == lead_y + 3 * lax.broadcasted_iota(jnp.int32, (cells, nest_cols), 0)
    ).astype(jnp.float32)
    r0, r1, r2, r3 = (current[STEPS + i, PAD:] for i in range(nest_rows))
    chosen = jnp.where(lead_x == 0, r0, jnp.where(lead_x == 1, r1, r2))
    feed[t, 0] = apply_table(pick, chosen)
    feed[t, 1] = apply_table(pick, r3)

    hi_count = nt // lo_count
    hi, lo = t // lo_count, lax.rem(t, lo_count)

    def feed_copy(source, target, slot):
        return remote(feed.at[source], feed.at[source], send4.at[slot], recv4.at[source], target, n)

    sends = []
    for step in range(1, hi_count):
        sends.append(feed_copy(t, lax.rem(hi + step, hi_count) * lo_count + lo, len(sends)))
        sends[-1].start()
    for step in range(1, lo_count):
        sends.append(feed_copy(t, hi * lo_count + lax.rem(lo + step, lo_count), len(sends)))
        sends[-1].start()

    nest_out[...] = current[STEPS:, PAD:]
    lax.fori_loop(marks[2], marks[3], parent_rows, 0)

    for step in range(1, hi_count):
        source = lax.rem(hi + step, hi_count) * lo_count + lo
        feed_copy(source, t, 0).wait_recv()
        for across in range(1, lo_count):
            target = hi * lo_count + lax.rem(lo + across, lo_count)
            sends.append(feed_copy(source, target, len(sends)))
            sends[-1].start()

    lax.fori_loop(marks[3], marks[4], parent_rows, 0)

    @pl.when(t > 0)
    def _():
        down_copy().wait_recv()

    @pl.when(t < nt - 1)
    def _():
        up_copy().wait_recv()

    @pl.when(n > 0)
    def _():
        right_copy().wait_recv()

    @pl.when(n < nn - 1)
    def _():
        left_copy().wait_recv()

    fresh[0] += KAPPA * above[...]
    fresh[tile_rows - 1] += KAPPA * below[...]
    fresh[:, 0] += KAPPA * beside[0]
    fresh[:, tile_cols - 1] += KAPPA * beside[1]

    for across in range(1, lo_count):
        for step in range(hi_count):
            source = lax.rem(hi + step, hi_count) * lo_count + lax.rem(lo + across, lo_count)
            feed_copy(source, t, 0).wait_recv()

    for copy in sends:
        copy.wait_send()
    for r in range(nt):
        @pl.when(t != r)
        def _():
            gather_copy(t, r).wait_send()

        @pl.when(t == r)
        def _():
            for q in range(nt):
                if q != r and needs(r, q):
                    spread_copy(r, q).wait_send()

    @pl.when(t < nt - 1)
    def _():
        halo_copy().wait_send()
        down_copy().wait_send()

    @pl.when(t > 0)
    def _():
        up_copy().wait_send()

    @pl.when(n < nn - 1)
    def _():
        right_copy().wait_send()

    @pl.when(n > 0)
    def _():
        left_copy().wait_send()


def feedback_kernel(
    nest_rows, nest_total, nest_cols, pos, fresh, feed, nest, out, nest_out, patch, store, patched
):
    tile_rows, cols, width = fresh.shape
    share = tile_rows // LOADS
    copies = [
        pltpu.make_async_copy(
            fresh.at[pl.ds(i * share, share)], out.at[pl.ds(i * share, share)], store.at[i]
        )
        for i in range(LOADS)
    ]
    copies.append(pltpu.make_async_copy(nest, nest_out.at[0], store.at[LOADS]))
    for copy in copies:
        copy.start()
    lead_x = lax.rem(3 - lax.rem(pos[0, 0], 3), 3)
    lead_y = lax.rem(3 - lax.rem(pos[0, 1], 3), 3)
    top = (pos[0, 0] + lead_x) // 3 - lax.axis_index("tiles") * tile_rows
    first_col = (pos[0, 1] + lead_y) // 3 - lax.axis_index("nests") * cols
    window = patch.shape[1]
    base_col = pl.multiple_of(jnp.clip(first_col // 8 * 8, 0, cols - window), 8)
    offset = first_col - base_col
    limit = (nest_cols - lead_y + 2) // 3
    cell = lax.broadcasted_iota(jnp.int32, (window, width), 0) - offset
    live = (cell >= 0) & (cell < limit)

    def fed(k):
        return (lead_x + 3 * k < nest_total) & (top + k >= 0) & (top + k < tile_rows)

    def patch_copy(k):
        return pltpu.make_async_copy(
            patch.at[k], out.at[top + k, pl.ds(base_col, window)], patched.at[k]
        )

    for k in range(patch.shape[0]):
        @pl.when(fed(k))
        def _():
            x = lead_x + 3 * k
            sender = x // nest_rows
            slot = (x - sender * nest_rows) // 3
            values = jnp.concatenate(
                [feed[sender, slot], jnp.zeros((8, width), jnp.float32)], axis=0
            )
            values = pltpu.roll(values, offset, 0)
            old = fresh[top + k, pl.ds(base_col, window)]
            patch[k] = jnp.where(live, old + 0.5 * (values - old), old)

    for copy in copies:
        copy.wait()
    for k in range(patch.shape[0]):
        @pl.when(fed(k))
        def _():
            patch_copy(k).start()
    for k in range(patch.shape[0]):
        @pl.when(fed(k))
        def _():
            patch_copy(k).wait()


def shards(nt, nn, parent, nest_state, parent_mix, nest_mix, courant, nest_pos):
    tile_rows, tile_cols, width = parent.shape
    _, nest_rows, nest_cols, _ = nest_state.shape
    nest_total = nest_rows * nt
    win = (nest_total + 1) // 3 + 2
    need = (nest_cols + 1) // 3 + 2
    span = -(-need // LANES) * LANES
    groups = span // LANES
    count = -(-(nest_rows + STEPS + 1) // 3) + 2
    fb_cols = -(-((nest_cols + 2) // 3) // LANES) * LANES
    lo_count = nt // 4
    slots = (nest_rows + 2) // 3
    part_rows = -(-win // (nt // lo_count))
    part_cols = -(-groups // lo_count) * LANES
    vmem = pl.BlockSpec(memory_space=pltpu.VMEM)
    smem = pl.BlockSpec(memory_space=pltpu.SMEM)
    hbm = pl.BlockSpec(memory_space=pltpu.HBM)
    f32 = jnp.float32
    dma = pltpu.SemaphoreType.DMA
    nest_pos, parent, nest_state, parent_mix, nest_mix, courant = (
        pltpu.with_memory_space_constraint(array, pltpu.HBM)
        for array in (nest_pos, parent, nest_state, parent_mix, nest_mix, courant)
    )
    nest_new, feed, parent_new = pl.pallas_call(
        functools.partial(exchange_kernel, nt, nn, lo_count),
        out_shape=(
            jax.ShapeDtypeStruct((nest_rows, nest_cols, width), f32),
            jax.ShapeDtypeStruct((nt, slots, fb_cols, width), f32),
            pltpu.VMEM(parent.shape, f32),
        ),
        in_specs=[smem] + [hbm] * 5,
        out_specs=(vmem, vmem, vmem),
        scratch_shapes=[
            pltpu.VMEM((tile_rows + 2, tile_cols + 2 * PAD, width), f32),
            pltpu.VMEM((win, span, width), f32),
            pltpu.VMEM((2, tile_rows, width), f32),
            pltpu.VMEM((tile_cols, width), f32),
            pltpu.VMEM((tile_cols, width), f32),
            pltpu.VMEM((2, tile_rows, width), f32),
            pltpu.VMEM((nest_rows, nest_cols, width), f32),
            pltpu.VMEM((width, width), f32),
            pltpu.VMEM((width, width), f32),
            pltpu.VMEM((2, width), f32),
            pltpu.VMEM((nt, part_rows, part_cols, width), f32),
            pltpu.VMEM((part_rows, part_cols, width), f32),
            pltpu.VMEM((count, span, width), f32),
            pltpu.VMEM((STEPS, nest_cols, width), f32),
            pltpu.VMEM((nest_rows + STEPS, nest_cols + PAD, width), f32),
            dma((LOADS + 4,)),
            dma((nt,)), dma((nt,)), dma((nt,)), dma((nt,)),
            dma((5,)), dma((5,)), dma((nt - 1,)), dma((nt,)),
        ],
        compiler_params=pltpu.CompilerParams(
            collective_id=0, has_side_effects=True, vmem_limit_bytes=VMEM_LIMIT
        ),
        name="nest_exchange",
    )(nest_pos, parent, nest_state, parent_mix, nest_mix, courant)

    fed_rows = (nest_total + 2) // 3
    parent_new = pltpu.with_memory_space_constraint(parent_new, pltpu.VMEM)
    return pl.pallas_call(
        functools.partial(feedback_kernel, nest_rows, nest_total, nest_cols),
        out_shape=(
            jax.ShapeDtypeStruct(parent.shape, f32),
            jax.ShapeDtypeStruct(nest_state.shape, f32),
        ),
        in_specs=[smem, vmem, vmem, vmem],
        out_specs=(hbm, hbm),
        scratch_shapes=[
            pltpu.VMEM((fed_rows, fb_cols + 8, width), f32),
            dma((LOADS + 1,)), dma((fed_rows,)),
        ],
        compiler_params=pltpu.CompilerParams(vmem_limit_bytes=FEED_LIMIT),
        name="feedback",
    )(nest_pos, parent_new, feed, nest_new)


def solution(mesh):
    placed = (
        P("tiles", "nests", None),
        P("nests", "tiles", None, None),
        P(),
        P(),
        P(),
        P("nests", None),
    )
    return jax.shard_map(
        functools.partial(shards, mesh.shape["tiles"], mesh.shape["nests"]),
        mesh=mesh,
        in_specs=placed,
        out_specs=(P("tiles", "nests", None), P("nests", "tiles", None, None)),
        check_vma=False,
    )
```
